256 devices in a mesh: gx: 16 (over z, core), gy: 16 (over y, x).
Axes of the slice: x: 4, y: 4, z: 8, core: 2. Of those that a mesh axis runs over, the one named last changes fastest.
Arguments:
- forward_state: float32 [9, 4, 256, 2048], P(None, None, 'gx', 'gy'), may hold values from -22 to 22
- adjoint_state: float32 [9, 4, 256, 2048], P(None, None, 'gx', 'gy'), may hold values from -22 to 22
- phase_labels: int32 [4, 256, 2048], P(None, 'gx', 'gy'), may hold values from 0 to 3
- phase_table: float32 [3, 4], replicated, may hold values from 0.5 to 1.5
- source_cells: int32 [512], replicated, may hold values from 0 to 2097151
- wavelet: float32 [4, 512], replicated, may hold values from -24 to 24
- receiver_cells: int32 [1024], replicated, may hold values from 0 to 2097151
- residual_traces: float32 [4, 1024], replicated, may hold values from -24 to 24
Outputs:
- adjoint_final: float32 [9, 4, 256, 2048], P(None, None, 'gx', 'gy')
- grad_lambda: float32 [4, 256, 2048], P(None, 'gx', 'gy')
- grad_mu: float32 [4, 256, 2048], P(None, 'gx', 'gy')
The draws below stay inside these ranges and needn't reach their ends.
All inputs are finite; a program needn't handle non-finite values.
Results may differ from the reference program's by a relative error of at most 0.00002.
Values sent between devices are 32-bit elements; how exact they have to be, the bound alone decides.
A program may use at most 128 MiB of HBM per device.

```python
import jax
import jax.numpy as jnp
from jax import lax

NZ = 4
ITERS = 4
PHASES = 4
NX = 256
NY = 2048
NSRC = 512
NREC = 1024


def grid_envelope():
    along_z = jnp.sin(jnp.pi * (jnp.arange(NZ, dtype=jnp.float32) + 0.5) / NZ)
    along_x = jnp.sin(jnp.pi * (jnp.arange(NX, dtype=jnp.float32) + 0.5) / NX)
    along_y = jnp.sin(jnp.pi * (jnp.arange(NY, dtype=jnp.float32) + 0.5) / NY)
    return along_z[:, None, None] * along_x[None, :, None] * along_y[None, None, :]


def plane_waves(key, count):
    keys = jax.random.split(key, 4)
    period_x = jax.random.randint(keys[0], (9, count), 12, 41)
    period_y = jax.random.randint(keys[1], (9, count), 12, 41)
    shift_x = jax.random.randint(keys[2], (9, count), 0, 40)
    shift_y = jax.random.randint(keys[3], (9, count), 0, 40)
    cells_x = jnp.arange(NX, dtype=jnp.int32)
    cells_y = jnp.arange(NY, dtype=jnp.int32)
    total = jnp.zeros((9, NX, NY), jnp.float32)
    for number in range(count):
        span_x = period_x[:, number:number + 1]
        span_y = period_y[:, number:number + 1]
        phase_x = ((cells_x[None, :] + shift_x[:, number:number + 1]) % span_x).astype(jnp.float32) / span_x.astype(jnp.float32)
        phase_y = ((cells_y[None, :] + shift_y[:, number:number + 1]) % span_y).astype(jnp.float32) / span_y.astype(jnp.float32)
        total = total + jnp.sin(2.0 * jnp.pi * phase_x)[:, :, None] * jnp.cos(2.0 * jnp.pi * phase_y)[:, None, :]
    return total[:, None, :, :]


def draw_forward_state(key, part):
    key = jax.random.fold_in(key, 11)
    smooth_key, rough_key = jax.random.split(key)
    waves = plane_waves(smooth_key, 3)
    envelope = grid_envelope()[None]
    smooth = 6.0 * envelope * waves
    rough = jnp.clip(jax.random.normal(rough_key, (9, NZ, NX, NY), jnp.float32), -4.0, 4.0)
    return smooth + rough


def draw_adjoint_state(key, part):
    key = jax.random.fold_in(key, 23)
    smooth_key, rough_key = jax.random.split(key)
    waves = plane_waves(smooth_key, 3)
    envelope = grid_envelope()[None]
    smooth = 6.0 * envelope * waves
    rough = jnp.clip(jax.random.normal(rough_key, (9, NZ, NX, NY), jnp.float32), -4.0, 4.0)
    return smooth + rough


def with_ends(drawn, stream_key, smallest, high):
    extent = drawn.shape
    place = [jax.random.randint(jax.random.fold_in(stream_key, axis), (), 0, extent[axis]) for axis in range(len(extent))]
    drawn = drawn.at[tuple(place)].set(smallest)
    longest = extent.index(max(extent))
    place[longest] = (place[longest] + 1) % extent[longest]
    return drawn.at[tuple(place)].set(high)


def scatter_about(stream_key, dims, width, reach, kind=jnp.bfloat16):
    array = width * jax.random.normal(stream_key, dims, jnp.float32)
    return jnp.clip(array, min=-reach, max=reach).astype(kind)


def setup_inputs(seed: int = 0) -> dict:
    streams_of = jax.random.split(jax.random.key(seed), 9)
    return {
        "forward_state": draw_forward_state(jax.random.fold_in(streams_of[8], 71), 0),
        "adjoint_state": draw_adjoint_state(jax.random.fold_in(streams_of[8], 71), 0),
        "phase_labels": with_ends(jax.random.randint(streams_of[2], (NZ, NX, NY), 0, PHASES), jax.random.fold_in(streams_of[2], 1), 0, PHASES - 1).astype(jnp.int32),
        "phase_table": jnp.clip(jax.random.uniform(streams_of[3], (3, PHASES), jnp.float32, 0.5, 1.5), 0.5, 1.5),
        "source_cells": with_ends(jax.random.randint(streams_of[4], (NSRC,), 0, NZ * NX * NY), jax.random.fold_in(streams_of[4], 1), 0, (NZ * NX * NY) - 1).astype(jnp.int32),
        "wavelet": scatter_about(streams_of[5], (ITERS, NSRC), 4.0, 24.0, jnp.float32),
        "receiver_cells": with_ends(jax.random.randint(streams_of[6], (NREC,), 0, NZ * NX * NY), jax.random.fold_in(streams_of[6], 1), 0, (NZ * NX * NY) - 1).astype(jnp.int32),
        "residual_traces": scatter_about(streams_of[7], (ITERS, NREC), 4.0, 24.0, jnp.float32),
    }


coeffs = (1225.0 / 1024.0, -245.0 / 3072.0, 49.0 / 5120.0, -5.0 / 7168.0)
step_dt = 0.1


def shift_diff(field, axis, plus):
    length = field.shape[axis] - 8
    total = jnp.zeros(field.shape[:axis] + (length,) + field.shape[axis + 1:], jnp.float32)
    for k in range(1, 5):
        first = 4 + k if plus else 3 + k
        second = 5 - k if plus else 4 - k
        total = total + coeffs[k - 1] * (lax.slice_in_dim(field, first, first + length, axis=axis) - lax.slice_in_dim(field, second, second + length, axis=axis))
    return total


def deriv(field, axis, plus):
    if axis == 0:
        padded = jnp.pad(field, ((4, 4), (0, 0), (0, 0)))
        return shift_diff(padded, 0, plus)[:, 4:-4, 4:-4]
    if axis == 1:
        return shift_diff(field, 1, plus)[:, :, 4:-4]
    return shift_diff(field, 2, plus)[:, 4:-4, :]


def divergence(stress_list):
    sxx, syy, szz, sxy, sxz, syz = stress_list
    return [deriv(sxx, 1, True) + deriv(sxy, 2, False) + deriv(sxz, 0, False),
            deriv(sxy, 1, False) + deriv(syy, 2, True) + deriv(syz, 0, False),
            deriv(sxz, 1, False) + deriv(syz, 2, False) + deriv(szz, 0, True)]


def strains(vel_list):
    vx, vy, vz = vel_list
    return [deriv(vx, 1, False), deriv(vy, 2, False), deriv(vz, 0, False),
            deriv(vx, 2, True) + deriv(vy, 1, True),
            deriv(vx, 0, True) + deriv(vz, 1, True),
            deriv(vy, 0, True) + deriv(vz, 2, True)]


def stress_inc(strain_list, lam, shear):
    trace = strain_list[0] + strain_list[1] + strain_list[2]
    normal = [lam * trace + 2.0 * shear * strain_list[i] for i in range(3)]
    return normal + [shear * strain_list[i] for i in range(3, 6)]


def materials(labels, table):
    lam = jnp.zeros(labels.shape, jnp.float32)
    shear = jnp.zeros(labels.shape, jnp.float32)
    dense = jnp.zeros(labels.shape, jnp.float32)
    for phase in range(table.shape[1]):
        match = labels == phase
        lam = lam + jnp.where(match, table[0, phase], 0.0)
        shear = shear + jnp.where(match, table[1, phase], 0.0)
        dense = dense + jnp.where(match, table[2, phase], 0.0)
    return lam, shear, 1.0 / dense


def pad_rim(field):
    return jnp.pad(field, ((0, 0), (4, 4), (4, 4)))


def reference(forward_state, adjoint_state, phase_labels, phase_table, source_cells, wavelet, receiver_cells, residual_traces):
    lam, shear, buoy = materials(phase_labels, phase_table)
    plane = NX * NY
    src_z, src_x, src_y = source_cells // plane, (source_cells // NY) % NX, source_cells % NY
    rec_z, rec_x, rec_y = receiver_cells // plane, (receiver_cells // NY) % NX, receiver_cells % NY
    vel = [forward_state[i] for i in range(3)]
    stress = [forward_state[i] for i in range(3, 9)]
    saved = []
    for step in range(ITERS):
        div = divergence([pad_rim(f) for f in stress])
        vel = [vel[i] + step_dt * buoy * div[i] for i in range(3)]
        vel[2] = vel[2].at[src_z, src_x, src_y].add(step_dt * wavelet[step])
        strain_now = strains([pad_rim(f) for f in vel])
        inc = stress_inc(strain_now, lam, shear)
        stress = [stress[i] + step_dt * inc[i] for i in range(6)]
        saved.append(strain_now)
    adj_vel = [adjoint_state[i] for i in range(3)]
    adj_stress = [adjoint_state[i] for i in range(3, 9)]
    grad_lambda = jnp.zeros(phase_labels.shape, jnp.float32)
    grad_mu = jnp.zeros(phase_labels.shape, jnp.float32)
    for step in range(ITERS):
        adj_strain = strains([pad_rim(f) for f in adj_vel])
        inc = stress_inc(adj_strain, lam, shear)
        adj_stress = [adj_stress[i] - step_dt * inc[i] for i in range(6)]
        div = divergence([pad_rim(f) for f in adj_stress])
        adj_vel = [adj_vel[i] - step_dt * buoy * div[i] for i in range(3)]
        adj_vel[2] = adj_vel[2].at[rec_z, rec_x, rec_y].add(step_dt * residual_traces[step])
        fwd = saved[ITERS - 1 - step]
        trace_f = fwd[0] + fwd[1] + fwd[2]
        trace_a = adj_strain[0] + adj_strain[1] + adj_strain[2]
        grad_lambda = grad_lambda + step_dt * trace_f * trace_a
        pair = 2.0 * (fwd[0] * adj_strain[0] + fwd[1] * adj_strain[1] + fwd[2] * adj_strain[2])
        pair = pair + fwd[3] * adj_strain[3] + fwd[4] * adj_strain[4] + fwd[5] * adj_strain[5]
        grad_mu = grad_mu + step_dt * pair
    return jnp.stack(adj_vel + adj_stress), grad_lambda, grad_mu
```

```python
import functools

import jax
import jax.numpy as jnp
from jax import lax
from jax.experimental import pallas as pl
from jax.experimental.pallas import tpu as pltpu
from jax.sharding import PartitionSpec as P

coeffs = (1225.0 / 1024.0, -245.0 / 3072.0, 49.0 / 5120.0, -5.0 / 7168.0)
step_dt = 0.1
MESH = pl.DeviceIdType.MESH

REACH = 4
BASE = 8
LANES = 128
SUB = 8
GROUP = 2 * REACH
PER_TILE = LANES // GROUP

STRESS_ORDER = (3, 6, 7, 4, 8, 5)
XX, XY, XZ, YY, YZ, ZZ = range(6)
X_SIDE, Y_SIDE = (0, 1), (2, 3)


def place_in_grid():
    gx, gy = lax.axis_index("gx"), lax.axis_index("gy")
    return gx, gy, lax.axis_size("gx"), lax.axis_size("gy")


def lane_of(shape):
    return lax.broadcasted_iota(jnp.int32, shape, len(shape) - 1)


def diff_x(buf, field, plus, rows):
    total = None
    for k in range(1, REACH + 1):
        first = BASE + (k if plus else k - 1)
        second = BASE + (1 - k if plus else -k)
        term = coeffs[k - 1] * (
            buf[field, :, first : first + rows, :] - buf[field, :, second : second + rows, :]
        )
        total = term if total is None else total + term
    return total


def shifted_y(field, halo, by):
    if by == 0:
        return field
    lane = lane_of(field.shape)
    if by > 0:
        return pltpu.roll(jnp.where(lane < by, halo, field), LANES - by, 2)
    return pltpu.roll(jnp.where(lane >= LANES + by, halo, field), -by, 2)


def diff_y(field, halo, plus):
    total = None
    for k in range(1, REACH + 1):
        first = k if plus else k - 1
        second = 1 - k if plus else -k
        term = coeffs[k - 1] * (shifted_y(field, halo, first) - shifted_y(field, halo, second))
        total = term if total is None else total + term
    return total


def diff_z(field, plus):
    layers = field.shape[0]
    out = []
    for i in range(layers):
        total = None
        for k in range(1, REACH + 1):
            first = i + (k if plus else k - 1)
            second = i + (1 - k if plus else -k)
            has_first, has_second = 0 <= first < layers, 0 <= second < layers
            if has_first and has_second:
                term = coeffs[k - 1] * (field[first] - field[second])
            elif has_first:
                term = coeffs[k - 1] * field[first]
            elif has_second:
                term = -coeffs[k - 1] * field[second]
            else:
                continue
            total = term if total is None else total + term
        out.append(jnp.zeros_like(field[0]) if total is None else total)
    return jnp.stack(out)


def pack_edges(fields, out_ref):
    layers, rows = fields[0].shape[:2]
    group = lane_of((SUB, LANES)) // GROUP
    tiles = [f[z, r : r + SUB] for f in fields for z in range(layers) for r in range(0, rows, SUB)]
    for start in range(0, len(tiles), PER_TILE):
        packed = jnp.zeros((SUB, LANES), jnp.float32)
        for j, tile in enumerate(tiles[start : start + PER_TILE]):
            packed = jnp.where(group == j, pltpu.roll(tile, (REACH + GROUP * j) % LANES, 1), packed)
        out_ref[start // PER_TILE] = packed


def unpack_edges(low_ref, high_ref, count, layers, rows):
    low_lane = lane_of((SUB, LANES)) % GROUP < REACH
    merged = [
        jnp.where(low_lane, low_ref[i], high_ref[i]) for i in range(low_ref.shape[0])
    ]
    pieces = []
    for j in range(count * layers * (rows // SUB)):
        back = (LANES - REACH - GROUP * (j % PER_TILE)) % LANES
        pieces.append(pltpu.roll(merged[j // PER_TILE], back, 1))
    per_layer = rows // SUB
    halos = []
    for f in range(count):
        halo_layers = []
        for z in range(layers):
            at = (f * layers + z) * per_layer
            halo_layers.append(jnp.concatenate(pieces[at : at + per_layer], axis=0))
        halos.append(jnp.stack(halo_layers))
    return halos


class Exchange:
    def __init__(self, kind, buf, packed, landed, send_sem, recv_sem, rows):
        self.kind, self.buf, self.packed, self.landed = kind, buf, packed, landed
        self.send_sem, self.recv_sem, self.rows = send_sem, recv_sem, rows

    def copies(self):
        gx, gy, nx, ny = place_in_grid()
        kind, end = self.kind, BASE + self.rows

        def rows_of(at):
            return self.buf.at[pl.ds(0, 3), :, pl.ds(at, REACH), :]

        def copy(side, src, dst, axis, to):
            return pltpu.make_async_remote_copy(
                src_ref=src,
                dst_ref=dst,
                send_sem=self.send_sem.at[kind, side],
                recv_sem=self.recv_sem.at[kind, side],
                device_id={axis: to},
                device_id_type=MESH,
            )

        return (
            (gx > 0, gx < nx - 1, copy(0, rows_of(BASE), rows_of(end), "gx", lax.rem(gx + nx - 1, nx))),
            (gx < nx - 1, gx > 0, copy(1, rows_of(end - REACH), rows_of(BASE - REACH), "gx", lax.rem(gx + 1, nx))),
            (gy > 0, gy < ny - 1, copy(2, self.packed.at[kind], self.landed.at[kind, 1], "gy", lax.rem(gy + ny - 1, ny))),
            (gy < ny - 1, gy > 0, copy(3, self.packed.at[kind], self.landed.at[kind, 0], "gy", lax.rem(gy + 1, ny))),
        )

    def start(self):
        for goes, _, copy in self.copies():
            pl.when(goes)(copy.start)

    def wait_recv(self):
        for _, arrives, copy in self.copies():
            pl.when(arrives)(copy.wait_recv)

    def wait_send(self):
        for goes, _, copy in self.copies():
            pl.when(goes)(copy.wait_send)


def own(buf, field, rows):
    return buf[field, :, BASE : BASE + rows, :]


def put(buf, field, rows, value):
    buf[field, :, BASE : BASE + rows, :] = value


def divergence(buf, halos, rows):
    sxy, syy, syz = (own(buf, i, rows) for i in (XY, YY, YZ))
    sxz, szz = own(buf, XZ, rows), own(buf, ZZ, rows)
    return (
        diff_x(buf, XX, True, rows) + diff_y(sxy, halos[0], False) + diff_z(sxz, False),
        diff_x(buf, XY, False, rows) + diff_y(syy, halos[1], True) + diff_z(syz, False),
        diff_x(buf, XZ, False, rows) + diff_y(syz, halos[2], False) + diff_z(szz, True),
    )


def strains(buf, halos, rows):
    vx, vy, vz = (own(buf, i, rows) for i in range(3))
    return (
        diff_x(buf, 0, False, rows),
        diff_y(vy, halos[1], False),
        diff_z(vz, False),
        diff_y(vx, halos[0], True) + diff_x(buf, 1, True, rows),
        diff_z(vx, True) + diff_x(buf, 2, True, rows),
        diff_z(vy, True) + diff_y(vz, halos[2], True),
    )


def log2(n):
    assert n > 0 and n & (n - 1) == 0
    return n.bit_length() - 1


def injections(cells_ref, traces_ref, out_ref, dims):
    layers, rows, nx_cells, ny_cells = dims
    gx, gy, _, _ = place_in_grid()
    steps, count = traces_ref.shape
    cells = cells_ref[...]
    layer = lax.shift_right_logical(cells, jnp.int32(log2(nx_cells * ny_cells)))
    at_x = (lax.shift_right_logical(cells, jnp.int32(log2(ny_cells))) & (nx_cells - 1)) - gx * rows
    at_y = (cells & (ny_cells - 1)) - gy * LANES
    here = (at_x >= 0) & (at_x < rows)
    row = jnp.where(here, layer * rows + at_x, -1)
    total = layers * rows
    row_hit = lax.broadcasted_iota(jnp.int32, (total, count), 0) == row
    lane_hit = lax.broadcasted_iota(jnp.int32, (LANES, count), 0) == at_y
    lanes = jnp.where(lane_hit, 1.0, 0.0).astype(jnp.bfloat16)
    for t in range(steps):
        rest = traces_ref[t : t + 1, :]
        field = None
        for _ in range(3):
            piece = rest.astype(jnp.bfloat16).astype(jnp.float32)
            rest = rest - piece
            spread = jnp.where(row_hit, piece, 0.0).astype(jnp.bfloat16)
            part = lax.dot_general(
                spread, lanes, (((1,), (1,)), ((), ())), preferred_element_type=jnp.float32
            )
            field = part if field is None else field + part
        out_ref[t] = (step_dt * field).reshape(layers, rows, LANES)


def kernel(
    dims,
    fwd_hbm, adj_hbm, labels_hbm, table_ref, src_ref, wav_ref, rec_ref, res_ref,
    out_hbm, gl_hbm, gm_hbm,
    fs, fv, aq, au, labels, mats, inj_f, inj_a, e_all, f_all, grads,
    packed, landed, in_sem, out_sem, send_sem, recv_sem,
):
    layers, rows = dims[0], dims[1]
    gx, gy, nx, ny = place_in_grid()
    steps = wav_ref.shape[0]

    edge = jnp.zeros((3, layers, REACH, LANES), jnp.float32)
    for buf in (fs, fv, aq, au):
        buf[0:3, :, BASE - REACH : BASE, :] = edge
        buf[0:3, :, BASE + rows : BASE + rows + REACH, :] = edge
    landed[...] = jnp.zeros_like(landed)

    barrier = pltpu.get_barrier_semaphore()
    for axis, here, size in (("gx", gx, nx), ("gy", gy, ny)):
        for to in (lax.rem(here + size - 1, size), lax.rem(here + 1, size)):
            pl.semaphore_signal(barrier, inc=1, device_id={axis: to}, device_id_type=MESH)

    loads = []

    def load(src, dst):
        copy = pltpu.make_async_copy(src, dst, in_sem.at[len(loads)])
        copy.start()
        loads.append(copy)

    own_rows = pl.ds(BASE, rows)
    for place, number in enumerate(STRESS_ORDER):
        load(fwd_hbm.at[number], fs.at[place, :, own_rows, :])
    load(adj_hbm.at[pl.ds(0, 3)], au.at[:, :, own_rows, :])
    first = len(loads)
    load(fwd_hbm.at[pl.ds(0, 3)], fv.at[:, :, own_rows, :])
    for place, number in enumerate(STRESS_ORDER):
        load(adj_hbm.at[number], aq.at[place, :, own_rows, :])
    load(labels_hbm, labels)

    def exchange(kind, buf):
        return Exchange(kind, buf, packed, landed, send_sem, recv_sem, rows)

    ex_s, ex_v, ex_u, ex_q = (exchange(i, b) for i, b in enumerate((fs, fv, au, aq)))

    def halos(ex):
        return unpack_edges(landed.at[ex.kind, 0], landed.at[ex.kind, 1], 3, layers, rows)

    for copy in loads[:first]:
        copy.wait()
    pack_edges([own(fs, i, rows) for i in (XY, YY, YZ)], packed.at[0])
    pack_edges([own(au, i, rows) for i in range(3)], packed.at[2])
    pl.semaphore_wait(barrier, 4)
    ex_s.start()
    ex_u.start()

    injections(src_ref, wav_ref, inj_f, dims)
    injections(rec_ref, res_ref, inj_a, dims)
    for copy in loads[first:]:
        copy.wait()
    label = labels[...]
    picked = []
    for prop in range(3):
        value = jnp.full(label.shape, table_ref[prop, 0])
        for phase in range(1, table_ref.shape[1]):
            value = jnp.where(label == phase, table_ref[prop, phase], value)
        picked.append(value)
    mats[0] = step_dt * picked[0]
    mats[1] = step_dt * picked[1]
    mats[2] = step_dt / picked[2]

    def stress_step(buf, strain, sign):
        exx, eyy, ezz, exy, exz, eyz = strain
        lam, shear = mats[0], mats[1]
        base, twice = lam * (exx + eyy + ezz), 2.0 * shear
        for place, inc in (
            (XX, base + twice * exx),
            (XY, shear * exy),
            (XZ, shear * exz),
            (YY, base + twice * eyy),
            (YZ, shear * eyz),
            (ZZ, base + twice * ezz),
        ):
            put(buf, place, rows, own(buf, place, rows) + sign * inc)

    def velocity_step(buf, div, sign, extra):
        buoy = mats[2]
        for i in range(3):
            new = own(buf, i, rows) + sign * (buoy * div[i])
            put(buf, i, rows, new + extra if i == 2 else new)

    def step(t, _):
        ex_s.wait_recv()
        div = divergence(fs, halos(ex_s), rows)
        pl.when(t > 0)(ex_v.wait_send)
        velocity_step(fv, div, 1.0, inj_f[t])
        pack_edges([own(fv, i, rows) for i in range(3)], packed.at[1])
        ex_v.start()
        ex_u.wait_recv()
        strain = strains(au, halos(ex_u), rows)
        for i in range(6):
            f_all[t, i] = strain[i]
        pl.when(t > 0)(ex_q.wait_send)
        stress_step(aq, strain, -1.0)
        pack_edges([own(aq, i, rows) for i in (XY, YY, YZ)], packed.at[3])
        ex_q.start()
        ex_v.wait_recv()
        strain = strains(fv, halos(ex_v), rows)
        for i in range(6):
            e_all[t, i] = strain[i]
        ex_s.wait_send()

        @pl.when(t < steps - 1)
        def _():
            stress_step(fs, [e_all[t, i] for i in range(6)], 1.0)
            pack_edges([own(fs, i, rows) for i in (XY, YY, YZ)], packed.at[0])
            ex_s.start()

        ex_q.wait_recv()
        div = divergence(aq, halos(ex_q), rows)
        ex_u.wait_send()
        velocity_step(au, div, -1.0, inj_a[t])

        @pl.when(t < steps - 1)
        def _():
            pack_edges([own(au, i, rows) for i in range(3)], packed.at[2])
            ex_u.start()

        return 0

    lax.fori_loop(0, steps, step, 0)
    ex_v.wait_send()
    ex_q.wait_send()

    stores = []

    def store(src, dst):
        copy = pltpu.make_async_copy(src, dst, out_sem.at[len(stores)])
        copy.start()
        stores.append(copy)

    store(au.at[:, :, own_rows, :], out_hbm.at[pl.ds(0, 3)])
    for place, number in enumerate(STRESS_ORDER):
        store(aq.at[place, :, own_rows, :], out_hbm.at[number])

    grad_l = grad_m = None
    for t in range(steps):
        e = [e_all[steps - 1 - t, i] for i in range(6)]
        f = [f_all[t, i] for i in range(6)]
        more_l = (e[0] + e[1] + e[2]) * (f[0] + f[1] + f[2])
        more_m = 2.0 * (e[0] * f[0] + e[1] * f[1] + e[2] * f[2])
        more_m = more_m + e[3] * f[3] + e[4] * f[4] + e[5] * f[5]
        grad_l = more_l if grad_l is None else grad_l + more_l
        grad_m = more_m if grad_m is None else grad_m + more_m
    grads[0] = step_dt * grad_l
    grads[1] = step_dt * grad_m
    store(grads.at[0], gl_hbm)
    store(grads.at[1], gm_hbm)
    for copy in stores:
        copy.wait()


def shards(fwd, adj, labels, table, src, wav, rec, res):
    _, layers, rows, lanes = fwd.shape
    assert lanes == LANES and rows % SUB == 0
    nx_cells, ny_cells = rows * lax.axis_size("gx"), lanes * lax.axis_size("gy")
    steps = wav.shape[0]
    dims = (layers, rows, nx_cells, ny_cells)
    tiles = -(-3 * layers * (rows // SUB) // PER_TILE)
    padded = rows + 2 * BASE
    f32 = jnp.float32
    block = (layers, rows, lanes)
    hbm = pl.BlockSpec(memory_space=pl.ANY)
    vmem = pl.BlockSpec(memory_space=pltpu.VMEM)
    smem = pl.BlockSpec(memory_space=pltpu.SMEM)
    return pl.pallas_call(
        functools.partial(kernel, dims),
        out_shape=(
            jax.ShapeDtypeStruct(fwd.shape, f32),
            jax.ShapeDtypeStruct(block, f32),
            jax.ShapeDtypeStruct(block, f32),
        ),
        in_specs=[hbm, hbm, hbm, smem, vmem, vmem, vmem, vmem],
        out_specs=(hbm, hbm, hbm),
        scratch_shapes=[
            pltpu.VMEM((6, layers, padded, lanes), f32),
            pltpu.VMEM((3, layers, padded, lanes), f32),
            pltpu.VMEM((6, layers, padded, lanes), f32),
            pltpu.VMEM((3, layers, padded, lanes), f32),
            pltpu.VMEM(block, jnp.int32),
            pltpu.VMEM((3,) + block, f32),
            pltpu.VMEM((steps,) + block, f32),
            pltpu.VMEM((steps,) + block, f32),
            pltpu.VMEM((steps, 6) + block, f32),
            pltpu.VMEM((steps, 6) + block, f32),
            pltpu.VMEM((2,) + block, f32),
            pltpu.VMEM((4, tiles, SUB, LANES), f32),
            pltpu.VMEM((4, 2, tiles, SUB, LANES), f32),
            pltpu.SemaphoreType.DMA((15,)),
            pltpu.SemaphoreType.DMA((9,)),
            pltpu.SemaphoreType.DMA((4, 4)),
            pltpu.SemaphoreType.DMA((4, 4)),
        ],
        compiler_params=pltpu.CompilerParams(
            collective_id=0, has_side_effects=True, vmem_limit_bytes=32 * 1024 * 1024
        ),
    )(fwd, adj, labels, table, src.reshape(1, -1), wav, rec.reshape(1, -1), res)


def solution(mesh):
    state, cells = P(None, None, "gx", "gy"), P(None, "gx", "gy")
    return jax.shard_map(
        shards,
        mesh=mesh,
        in_specs=(state, state, cells, P(), P(), P(), P(), P()),
        out_specs=(state, cells, cells),
        check_vma=False,
    )
```

```python
import functools

import jax
import jax.numpy as jnp
from jax import lax
from jax.experimental import pallas as pl
from jax.experimental.pallas import tpu as pltpu
from jax.sharding import PartitionSpec as P

coeffs = (1225.0 / 1024.0, -245.0 / 3072.0, 49.0 / 5120.0, -5.0 / 7168.0)
step_dt = 0.1
MESH = pl.DeviceIdType.MESH

LAYERS, ROWS, LANES, SUB = 4, 16, 128, 8
REACH = 4
BASE = 16
PADDED = ROWS + 2 * BASE
END = BASE + ROWS

FWD = (3, 6, 7, 4, 8, 5, 0, 1, 2)
ADJ = (0, 1, 2, 3, 6, 7, 4, 8, 5)
FWD_EDGES = tuple(range(9))
ADJ_EDGES = (0, 1, 2, 4, 6, 7)
FWD_CORNERS = (0, 1, 2, 3, 4)
ADJ_CORNERS = (0, 1)


def place_in_grid():
    gx, gy = lax.axis_index("gx"), lax.axis_index("gy")
    return gx, gy, lax.axis_size("gx"), lax.axis_size("gy")


def lane_of(shape):
    return lax.broadcasted_iota(jnp.int32, shape, len(shape) - 1)


def row_of(shape):
    return lax.broadcasted_iota(jnp.int32, shape, len(shape) - 2)


def roll(value, by):
    by %= LANES
    return value if by == 0 else pltpu.roll(value, by, value.ndim - 1)


def weighted(shift, plus):
    total = None
    for k in range(1, REACH + 1):
        first = k if plus else k - 1
        term = coeffs[k - 1] * (shift(first) - shift(first + 1 - 2 * k))
        total = term if total is None else total + term
    return total


def with_x_halo(buf, field, d=0):
    own = buf[field, :, BASE + d : END + d, :]
    after = buf[field, :, END + d : END + d + SUB, :]
    before = buf[field, :, BASE - SUB + d : BASE + d, :]
    halo = jnp.where(row_of(after.shape) < REACH, after, before)
    return jnp.concatenate([own, halo], axis=1)


def diff_x(buf, field, plus, wide):
    if wide:
        return weighted(lambda d: with_x_halo(buf, field, d), plus)
    return weighted(lambda d: buf[field, :, BASE + d : END + d, :], plus)


def diff_y(field, halo, plus):
    lane = lane_of(field.shape)

    def shift(d):
        if d == 0:
            return field
        return roll(jnp.where(lane < d if d > 0 else lane >= LANES + d, halo, field), -d)

    return weighted(shift, plus)


def diff_z(field, plus):
    out = []
    for i in range(LAYERS):
        total = None
        for k in range(1, REACH + 1):
            first = i + (k if plus else k - 1)
            second = first + 1 - 2 * k
            has_first, has_second = 0 <= first < LAYERS, 0 <= second < LAYERS
            if has_first and has_second:
                term = coeffs[k - 1] * (field[first] - field[second])
            elif has_first:
                term = coeffs[k - 1] * field[first]
            elif has_second:
                term = -coeffs[k - 1] * field[second]
            else:
                continue
            total = term if total is None else total + term
        out.append(total)
    return jnp.stack(out)


def strip_x(buf, field, plus):
    return weighted(lambda d: buf[field, BASE + d : END + d, :], plus)


def strip_y(field, plus):
    return weighted(lambda d: roll(field, -d), plus)


def strip_z(field, plus):
    layer = lane_of(field.shape) // 32
    weights = {}
    for k in range(1, REACH + 1):
        first = k if plus else k - 1
        weights[first] = weights.get(first, 0.0) + coeffs[k - 1]
        weights[first + 1 - 2 * k] = weights.get(first + 1 - 2 * k, 0.0) - coeffs[k - 1]
    total = None
    for d, weight in weights.items():
        if abs(d) >= LAYERS:
            continue
        inside = (layer + d >= 0) & (layer + d < LAYERS)
        term = jnp.where(inside, weight, 0.0) * roll(field, -32 * d)
        total = term if total is None else total + term
    return total


def pack_edge(field):
    group = lane_of((SUB, LANES)) // 16
    packed = None
    for z in range(LAYERS):
        for tile in range(2):
            at = 2 * z + tile
            piece = roll(field[z, SUB * tile : SUB * (tile + 1)], 8 + 16 * at)
            packed = piece if packed is None else jnp.where(group == at, piece, packed)
    return packed


def pack_corners(edges, out_ref, slot):
    group = lane_of((SUB, LANES)) // 8 % 4
    top = row_of((SUB, LANES)) < REACH
    for start in range(0, len(edges), 4):
        packed = None
        for g, edge in enumerate(edges[start : start + 4]):
            piece = jnp.where(top, roll(edge, 8 * g - 4), roll(edge, 8 * g - 20))
            packed = piece if packed is None else jnp.where(group == g, piece, packed)
        out_ref[slot, start // 4] = packed


def strip_of(edge, low, high):
    half = lane_of(edge.shape) % 16 < 8
    first, last = jnp.where(half, low, edge), jnp.where(half, edge, high)
    side = lane_of(edge.shape) % 32 < 16
    tiles = [jnp.where(side, first, roll(last, 16)), jnp.where(side, roll(first, -16), last)]
    return jnp.concatenate(tiles, axis=0)


def y_halo_of_edges(low, high):
    merged = jnp.where(lane_of(low.shape) % 16 < 8, low, high)
    return jnp.stack([
        jnp.concatenate([roll(merged, 120 - 32 * z - 16 * tile) for tile in range(2)], axis=0)
        for z in range(LAYERS)
    ])


def y_halo_of_strip(strip):
    merged = jnp.where(lane_of(strip.shape) % 16 < 8, strip, roll(strip, -16))
    return jnp.stack([roll(merged, 120 - 32 * z) for z in range(LAYERS)])


def y_halo_of_corners(corner, g):
    return jnp.stack([roll(corner, 124 - 32 * z - 8 * g) for z in range(LAYERS)])


def strip_rows_of_corners(corner, g):
    side = lane_of(corner.shape) % 32 < 16
    return jnp.where(side, roll(corner, 4 - 8 * g), roll(corner, 20 - 8 * g))


class Chain:
    def __init__(self, refs, deep, shallow, edges, corners):
        (self.buf, self.edge, self.side, self.corner, self.corners_in,
         self.strips, self.send_sem, self.recv_sem) = refs
        self.deep, self.shallow = deep, shallow
        self.edges, self.corner_places = edges, corners

    def copies(self, slot):
        gx, gy, nx, ny = place_in_grid()
        out = []

        def add(dx, dy, src, dst):
            def inside(sx, sy):
                conds = []
                if sx:
                    conds.append(gx > 0 if sx < 0 else gx < nx - 1)
                if sy:
                    conds.append(gy > 0 if sy < 0 else gy < ny - 1)
                return conds[0] if len(conds) == 1 else jnp.logical_and(*conds)

            copy = pltpu.make_async_remote_copy(
                src_ref=src,
                dst_ref=dst,
                send_sem=self.send_sem.at[slot, len(out)],
                recv_sem=self.recv_sem.at[slot, len(out)],
                device_id=(lax.rem(gx + dx + nx, nx), lax.rem(gy + dy + ny, ny)),
                device_id_type=MESH,
            )
            out.append((inside(dx, dy), inside(-dx, -dy), copy))

        for dx in (-1, 1):
            for dy in (-1, 1):
                at = (1 - dx) // 2 * 2 + (1 - dy) // 2
                add(dx, dy, self.corner.at[slot], self.corners_in.at[slot, at])
        for dy in (-1, 1):
            add(0, dy, self.edge.at[slot], self.side.at[slot, (1 - dy) // 2])
        for fields, count in ((self.deep, SUB), (self.shallow, REACH)):
            for dx in (-1, 1):
                src = BASE if dx < 0 else END - count
                dst = END if dx < 0 else BASE - count
                part = pl.ds(fields[0], len(fields))
                add(dx, 0, self.buf.at[slot, part, :, pl.ds(src, count), :],
                    self.buf.at[slot, part, :, pl.ds(dst, count), :])
        return out

    def clear(self):
        for slot in range(2):
            for fields, count in ((self.deep, SUB), (self.shallow, REACH)):
                zero = jnp.zeros((len(fields), LAYERS, count, LANES), jnp.float32)
                part = pl.ds(fields[0], len(fields))
                self.buf[slot, part, :, BASE - count : BASE, :] = zero
                self.buf[slot, part, :, END : END + count, :] = zero
        self.side[...] = jnp.zeros_like(self.side)
        self.corners_in[...] = jnp.zeros_like(self.corners_in)

    def send(self, slot):
        edges = {}
        for i, place in enumerate(self.edges):
            edges[place] = pack_edge(self.own(slot, place))
            self.edge[slot, i] = edges[place]
        pack_corners([edges[place] for place in self.corner_places], self.corner, slot)
        for goes, _, copy in self.copies(slot):
            pl.when(goes)(copy.start)

    def wait_recv(self, slot):
        for _, arrives, copy in self.copies(slot):
            pl.when(arrives)(copy.wait_recv)

    def wait_send(self, slot):
        for goes, _, copy in self.copies(slot):
            pl.when(goes)(copy.wait_send)

    def own(self, slot, place):
        return self.buf[slot, place, :, BASE:END, :]

    def put(self, slot, place, value):
        self.buf[slot, place, :, BASE:END, :] = value

    def strip(self, slot, place):
        i = self.edges.index(place)
        return strip_of(self.edge[slot, i], self.side[slot, 0, i], self.side[slot, 1, i])

    def y_halo(self, slot, place):
        i = self.edges.index(place)
        return y_halo_of_edges(self.side[slot, 0, i], self.side[slot, 1, i])

    def corner_tiles(self, slot):
        shape = (SUB, LANES)
        first, top = lane_of(shape) % 8 < 4, row_of(shape) < REACH
        out = []
        for i in range(self.corner.shape[1]):
            here = [self.corners_in[slot, at, i] for at in range(4)]
            out.append(jnp.where(top, jnp.where(first, here[2], here[3]),
                                 jnp.where(first, here[0], here[1])))
        return out

    def wide_y_halo(self, slot, place, tiles):
        at = self.corner_places.index(place)
        corner = y_halo_of_corners(tiles[at // 4], at % 4)
        return jnp.concatenate([self.y_halo(slot, place), corner], axis=1)

    def set_strip_rows(self, place, strip, tiles):
        at = self.corner_places.index(place)
        rows = strip_rows_of_corners(tiles[at // 4], at % 4)
        self.strips[place, BASE:END, :] = strip
        self.strips[place, BASE - SUB : BASE, :] = rows
        self.strips[place, END : END + SUB, :] = rows


def put_wide(work, place, value):
    work[place, :, BASE:END, :] = value[:, :ROWS]
    work[place, :, END : END + REACH, :] = value[:, ROWS : ROWS + REACH]
    work[place, :, BASE - REACH : BASE, :] = value[:, ROWS + REACH :]


def log2(n):
    assert n > 0 and n & (n - 1) == 0
    return n.bit_length() - 1


def spread(traces_ref, row, lane, rows, store):
    steps, count = traces_ref.shape
    row_hit = lax.broadcasted_iota(jnp.int32, (rows, count), 0) == row
    lane_hit = lax.broadcasted_iota(jnp.int32, (LANES, count), 0) == lane
    lanes = jnp.where(lane_hit, 1.0, 0.0).astype(jnp.bfloat16)
    for t in range(steps):
        rest = traces_ref[t : t + 1, :]
        total = None
        for _ in range(3):
            piece = rest.astype(jnp.bfloat16).astype(jnp.float32)
            rest = rest - piece
            left = jnp.where(row_hit, piece, 0.0).astype(jnp.bfloat16)
            part = lax.dot_general(
                left, lanes, (((1,), (1,)), ((), ())), preferred_element_type=jnp.float32
            )
            total = part if total is None else total + part
        store(t, step_dt * total)


def positions(cells_ref, nx_cells, ny_cells):
    gx, gy, _, _ = place_in_grid()
    cells = cells_ref[...]
    layer = lax.shift_right_logical(cells, jnp.int32(log2(nx_cells * ny_cells)))
    at_x = lax.shift_right_logical(cells, jnp.int32(log2(ny_cells))) & (nx_cells - 1)
    return layer, at_x - gx * ROWS, (cells & (ny_cells - 1)) - gy * LANES


def kernel(
    dims,
    fwd_hbm, adj_hbm, labels_hbm, table_ref, src_ref, wav_ref, rec_ref, res_ref,
    out_hbm, gl_hbm, gm_hbm,
    f_buf, f_edge, f_side, f_corner, f_corners_in, f_strips,
    a_buf, a_edge, a_side, a_corner, a_corners_in, a_strips,
    f_work, a_work, labels, lab, lab_edge, lab_side, mats, mats_s,
    inj_f, inj_s, inj_a, e_all, f_all, grads,
    in_sem, out_sem, f_send, f_recv, a_send, a_recv, l_send, l_recv,
):
    nx_cells, ny_cells = dims
    gx, gy, nx, ny = place_in_grid()
    steps = wav_ref.shape[0]

    fwd = Chain((f_buf, f_edge, f_side, f_corner, f_corners_in, f_strips, f_send, f_recv),
                (0, 1, 2), (3, 4, 5, 6, 7, 8), FWD_EDGES, FWD_CORNERS)
    adj = Chain((a_buf, a_edge, a_side, a_corner, a_corners_in, a_strips, a_send, a_recv),
                (0, 1, 2), (3, 4, 5), ADJ_EDGES, ADJ_CORNERS)

    fwd.clear()
    adj.clear()
    lab[...] = jnp.zeros_like(lab)
    lab_side[...] = jnp.zeros_like(lab_side)
    barrier = pltpu.get_barrier_semaphore()
    around = [(dx, dy) for dx in (-1, 0, 1) for dy in (-1, 0, 1) if dx or dy]
    for dx, dy in around:
        to = (lax.rem(gx + dx + nx, nx), lax.rem(gy + dy + ny, ny))
        pl.semaphore_signal(barrier, inc=1, device_id=to, device_id_type=MESH)

    loads = []

    def load(src, dst):
        copy = pltpu.make_async_copy(src, dst, in_sem.at[len(loads)])
        copy.start()
        loads.append(copy)

    own_rows = pl.ds(BASE, ROWS)
    load(labels_hbm, labels)
    for place, number in enumerate(FWD):
        load(fwd_hbm.at[number], f_buf.at[0, place, :, own_rows, :])
    for place, number in enumerate(ADJ):
        load(adj_hbm.at[number], a_buf.at[0, place, :, own_rows, :])

    loads[0].wait()
    lab[0, :, BASE:END, :] = labels[...].astype(jnp.float32)
    lab_edge[0] = pack_edge(lab[0, :, BASE:END, :])
    lab_copies = []
    for goes, arrives, src, dst, axis, to in (
        (gx > 0, gx < nx - 1, lab.at[0, :, pl.ds(BASE, REACH), :], lab.at[0, :, pl.ds(END, REACH), :], "gx", lax.rem(gx + nx - 1, nx)),
        (gx < nx - 1, gx > 0, lab.at[0, :, pl.ds(END - REACH, REACH), :], lab.at[0, :, pl.ds(BASE - REACH, REACH), :], "gx", lax.rem(gx + 1, nx)),
        (gy > 0, gy < ny - 1, lab_edge, lab_side.at[1], "gy", lax.rem(gy + ny - 1, ny)),
        (gy < ny - 1, gy > 0, lab_edge, lab_side.at[0], "gy", lax.rem(gy + 1, ny)),
    ):
        copy = pltpu.make_async_remote_copy(
            src_ref=src, dst_ref=dst, send_sem=l_send.at[len(lab_copies)],
            recv_sem=l_recv.at[len(lab_copies)], device_id={axis: to}, device_id_type=MESH,
        )
        lab_copies.append((goes, arrives, copy))

    for copy in loads[1:]:
        copy.wait()
    pl.semaphore_wait(barrier, len(around))
    fwd.send(0)
    adj.send(0)
    for goes, _, copy in lab_copies:
        pl.when(goes)(copy.start)

    layer, at_x, at_y = positions(src_ref, nx_cells, ny_cells)
    wide = ROWS + SUB
    here = jnp.where(at_x < 0, at_x + wide, at_x)
    row = jnp.where((at_x >= -REACH) & (at_x < ROWS + REACH), layer * wide + here, -1)

    def store_wide(t, value):
        inj_f[t] = value.reshape(LAYERS, wide, LANES)

    spread(wav_ref, row, at_y, LAYERS * wide, store_wide)
    column = jnp.where((at_y >= -REACH) & (at_y < 0), 32 * layer + 8 + at_y, -1)
    column = jnp.where((at_y >= LANES) & (at_y < LANES + REACH), 32 * layer + 24 + at_y - LANES, column)

    def store_strip(t, value):
        inj_s[t] = value

    spread(wav_ref, at_x, column, ROWS, store_strip)
    layer, at_x, at_y = positions(rec_ref, nx_cells, ny_cells)
    row = jnp.where((at_x >= 0) & (at_x < ROWS), layer * ROWS + at_x, -1)

    def store_own(t, value):
        inj_a[t] = value.reshape(LAYERS, ROWS, LANES)

    spread(res_ref, row, at_y, LAYERS * ROWS, store_own)

    for _, arrives, copy in lab_copies:
        pl.when(arrives)(copy.wait_recv)

    def materials(label, inside, out):
        for prop in range(3):
            value = jnp.full(label.shape, table_ref[prop, 0])
            for phase in range(1, table_ref.shape[1]):
                value = jnp.where(label == phase, table_ref[prop, phase], value)
            value = step_dt * value if prop < 2 else step_dt / value
            out[prop] = jnp.where(inside, value, 0.0)

    shape = (LAYERS, wide, LANES)
    r = row_of(shape)
    inside = (r < ROWS) | ((r < ROWS + REACH) & (gx < nx - 1)) | ((r >= ROWS + REACH) & (gx > 0))
    materials(with_x_halo(lab, 0), inside, mats)
    lane = lane_of((ROWS, LANES))
    column = lane % 16 + jnp.where(lane % 32 < 16, -8, LANES - 8)
    inside = ((column >= 0) | (gy > 0)) & ((column < LANES) | (gy < ny - 1))
    materials(strip_of(lab_edge[0], lab_side[0, 0], lab_side[1, 0]), inside, mats_s)

    def forward_step(t):
        slot = lax.rem(t, 2)
        other = 1 - slot
        buf = f_buf.at[slot]
        fwd.wait_recv(slot)
        tiles = fwd.corner_tiles(slot)
        div = []
        sxx, sxy, sxz, syy, syz, szz, vx, vy, vz = range(9)
        for first, second, third, plus in (
            (sxx, sxy, sxz, 0), (sxy, syy, syz, 1), (sxz, syz, szz, 2)
        ):
            div.append(
                diff_x(buf, first, plus == 0, True)
                + diff_y(with_x_halo(buf, second), fwd.wide_y_halo(slot, second, tiles), plus == 1)
                + diff_z(with_x_halo(buf, third), plus == 2)
            )
        strips = [fwd.strip(slot, place) for place in range(9)]
        for place in (sxx, sxy, sxz):
            fwd.set_strip_rows(place, strips[place], tiles)
        strip_div = [
            strip_x(f_strips, sxx, True) + strip_y(strips[sxy], False) + strip_z(strips[sxz], False),
            strip_x(f_strips, sxy, False) + strip_y(strips[syy], True) + strip_z(strips[syz], False),
            strip_x(f_strips, sxz, False) + strip_y(strips[syz], False) + strip_z(strips[szz], True),
        ]
        pl.when(t > 0)(lambda: fwd.wait_send(other))
        halos = []
        for i in range(3):
            new = with_x_halo(buf, vx + i) + mats[2] * div[i]
            side = strips[vx + i] + mats_s[2] * strip_div[i]
            if i == 2:
                new, side = new + inj_f[t], side + inj_s[t]
            put_wide(f_work, i, new)
            fwd.put(other, vx + i, new[:, :ROWS])
            halos.append(y_halo_of_strip(side))
        v = [fwd.own(other, vx + i) for i in range(3)]
        strain = (
            diff_x(f_work, 0, False, False),
            diff_y(v[1], halos[1], False),
            diff_z(v[2], False),
            diff_y(v[0], halos[0], True) + diff_x(f_work, 1, True, False),
            diff_z(v[0], True) + diff_x(f_work, 2, True, False),
            diff_z(v[1], True) + diff_y(v[2], halos[2], True),
        )
        for i in range(6):
            e_all[t, i] = strain[i]

        @pl.when(t < steps - 1)
        def _():
            lam, shear = mats[0, :, :ROWS], mats[1, :, :ROWS]
            exx, eyy, ezz, exy, exz, eyz = (e_all[t, i] for i in range(6))
            base, twice = lam * (exx + eyy + ezz), 2.0 * shear
            for place, inc in (
                (sxx, base + twice * exx), (sxy, shear * exy), (sxz, shear * exz),
                (syy, base + twice * eyy), (syz, shear * eyz), (szz, base + twice * ezz),
            ):
                fwd.put(other, place, fwd.own(slot, place) + inc)
            fwd.send(other)

    def adjoint_step(t):
        slot = lax.rem(t, 2)
        other = 1 - slot
        buf = a_buf.at[slot]
        adj.wait_recv(slot)
        tiles = adj.corner_tiles(slot)
        vx, vy, vz, sxx, sxy, sxz, syy, syz, szz = range(9)
        u = [with_x_halo(buf, i) for i in range(3)]
        u_halo = [adj.wide_y_halo(slot, i, tiles) for i in range(2)]
        u_own = adj.own(slot, vz)
        exx, eyy, ezz = diff_x(buf, vx, False, True), diff_y(u[1], u_halo[1], False), diff_z(u[2], False)
        exy = diff_y(u[0], u_halo[0], True) + diff_x(buf, vy, True, True)
        exz = diff_z(u[0], True) + diff_x(buf, vz, True, True)
        eyz = diff_z(adj.own(slot, vy), True) + diff_y(u_own, adj.y_halo(slot, vz), True)
        for i, value in enumerate((exx, eyy, ezz, exy, exz)):
            f_all[t, i] = value[:, :ROWS]
        f_all[t, 5] = eyz
        side = [adj.strip(slot, i) for i in range(3)]
        for i in range(2):
            adj.set_strip_rows(i, side[i], tiles)
        side_xx, side_yy, side_zz = strip_x(a_strips, vx, False), strip_y(side[1], False), strip_z(side[2], False)
        side_xy = strip_y(side[0], True) + strip_x(a_strips, vy, True)
        side_yz = strip_z(side[1], True) + strip_y(side[2], True)
        pl.when(t > 0)(lambda: adj.wait_send(other))
        lam, shear = mats[0], mats[1]
        base = lam * (exx + eyy + ezz)
        for i, (place, inc) in enumerate(
            ((sxx, base + 2.0 * shear * exx), (sxy, shear * exy), (sxz, shear * exz))
        ):
            new = with_x_halo(buf, place) - inc
            put_wide(a_work, i, new)
            adj.put(other, place, new[:, :ROWS])
        base, shear = base[:, :ROWS], shear[:, :ROWS]
        for place, inc in (
            (syy, base + 2.0 * shear * eyy[:, :ROWS]),
            (syz, shear * eyz),
            (szz, base + 2.0 * shear * ezz[:, :ROWS]),
        ):
            adj.put(other, place, adj.own(slot, place) - inc)
        lam, shear = mats_s[0], mats_s[1]
        side_inc = {
            sxy: shear * side_xy,
            syy: lam * (side_xx + side_yy + side_zz) + 2.0 * shear * side_yy,
            syz: shear * side_yz,
        }
        halo = {
            place: y_halo_of_strip(adj.strip(slot, place) - inc) for place, inc in side_inc.items()
        }
        new = {place: adj.own(other, place) for place in (sxy, sxz, syy, syz, szz)}
        div = (
            diff_x(a_work, 0, True, False) + diff_y(new[sxy], halo[sxy], False) + diff_z(new[sxz], False),
            diff_x(a_work, 1, False, False) + diff_y(new[syy], halo[syy], True) + diff_z(new[syz], False),
            diff_x(a_work, 2, False, False) + diff_y(new[syz], halo[syz], False) + diff_z(new[szz], True),
        )
        buoy = mats[2, :, :ROWS]
        for i in range(3):
            value = adj.own(slot, i) - buoy * div[i]
            adj.put(other, i, value + inj_a[t] if i == 2 else value)
        pl.when(t < steps - 1)(lambda: adj.send(other))

    def step(t, _):
        forward_step(t)
        adjoint_step(t)
        return 0

    lax.fori_loop(0, steps, step, 0)
    last = (steps - 1) % 2
    fwd.wait_send(last)
    adj.wait_send(last)
    for goes, _, copy in lab_copies:
        pl.when(goes)(copy.wait_send)

    stores = []

    def store(src, dst):
        copy = pltpu.make_async_copy(src, dst, out_sem.at[len(stores)])
        copy.start()
        stores.append(copy)

    for place, number in enumerate(ADJ):
        store(a_buf.at[1 - last, place, :, own_rows, :], out_hbm.at[number])

    grad_l = grad_m = None
    for t in range(steps):
        e = [e_all[steps - 1 - t, i] for i in range(6)]
        f = [f_all[t, i] for i in range(6)]
        more_l = (e[0] + e[1] + e[2]) * (f[0] + f[1] + f[2])
        more_m = 2.0 * (e[0] * f[0] + e[1] * f[1] + e[2] * f[2])
        more_m = more_m + e[3] * f[3] + e[4] * f[4] + e[5] * f[5]
        grad_l = more_l if grad_l is None else grad_l + more_l
        grad_m = more_m if grad_m is None else grad_m + more_m
    grads[0] = step_dt * grad_l
    grads[1] = step_dt * grad_m
    store(grads.at[0], gl_hbm)
    store(grads.at[1], gm_hbm)
    for copy in stores:
        copy.wait()


def shards(fwd, adj, labels, table, src, wav, rec, res):
    assert labels.shape == (LAYERS, ROWS, LANES)
    dims = (ROWS * lax.axis_size("gx"), LANES * lax.axis_size("gy"))
    steps = wav.shape[0]
    f32 = jnp.float32
    block, tile = (LAYERS, ROWS, LANES), (SUB, LANES)
    wide = (LAYERS, ROWS + SUB, LANES)

    def vmem(*shape):
        return pltpu.VMEM(shape, f32)

    def chain(edges, corners, strips):
        return [
            vmem(2, 9, LAYERS, PADDED, LANES),
            vmem(2, edges, *tile),
            vmem(2, 2, edges, *tile),
            vmem(2, corners, *tile),
            vmem(2, 4, corners, *tile),
            vmem(strips, PADDED, LANES),
        ]

    in_hbm = pl.BlockSpec(memory_space=pl.ANY)
    in_vmem = pl.BlockSpec(memory_space=pltpu.VMEM)
    in_smem = pl.BlockSpec(memory_space=pltpu.SMEM)
    dma = pltpu.SemaphoreType.DMA
    return pl.pallas_call(
        functools.partial(kernel, dims),
        out_shape=(
            jax.ShapeDtypeStruct(fwd.shape, f32),
            jax.ShapeDtypeStruct(block, f32),
            jax.ShapeDtypeStruct(block, f32),
        ),
        in_specs=[in_hbm, in_hbm, in_hbm, in_smem, in_vmem, in_vmem, in_vmem, in_vmem],
        out_specs=(in_hbm, in_hbm, in_hbm),
        scratch_shapes=chain(9, 2, 3) + chain(6, 1, 2) + [
            vmem(3, LAYERS, PADDED, LANES),
            vmem(3, LAYERS, PADDED, LANES),
            pltpu.VMEM(block, jnp.int32),
            vmem(1, LAYERS, PADDED, LANES),
            vmem(1, *tile),
            vmem(2, 1, *tile),
            vmem(3, *wide),
            vmem(3, ROWS, LANES),
            vmem(steps, *wide),
            vmem(steps, ROWS, LANES),
            vmem(steps, *block),
            vmem(steps, 6, *block),
            vmem(steps, 6, *block),
            vmem(2, *block),
            dma((19,)), dma((11,)),
            dma((2, 10)), dma((2, 10)), dma((2, 10)), dma((2, 10)),
            dma((4,)), dma((4,)),
        ],
        compiler_params=pltpu.CompilerParams(
            collective_id=0, has_side_effects=True, vmem_limit_bytes=62 * 1024 * 1024
        ),
    )(fwd, adj, labels, table, src.reshape(1, -1), wav, rec.reshape(1, -1), res)


def solution(mesh):
    state, cells = P(None, None, "gx", "gy"), P(None, "gx", "gy")
    return jax.shard_map(
        shards,
        mesh=mesh,
        in_specs=(state, state, cells, P(), P(), P(), P(), P()),
        out_specs=(state, cells, cells),
        check_vma=False,
    )
```

```python
import functools

import jax
import jax.numpy as jnp
from jax import lax
from jax.experimental import pallas as pl
from jax.experimental.pallas import tpu as pltpu
from jax.sharding import PartitionSpec as P

coeffs = (1225.0 / 1024.0, -245.0 / 3072.0, 49.0 / 5120.0, -5.0 / 7168.0)
step_dt = 0.1
MESH = pl.DeviceIdType.MESH

LAYERS, ROWS, LANES, SUB = 4, 16, 128, 8
REACH = 4
BASE = 16
PADDED = ROWS + 2 * BASE
END = BASE + ROWS

FWD = (3, 6, 7, 4, 8, 5, 0, 1, 2)
ADJ = (0, 1, 2, 3, 6, 7, 4, 8, 5)
FWD_EDGES = tuple(range(9))
ADJ_EDGES = (0, 1, 2, 4, 6, 7)
FWD_CORNERS = (0, 1, 2, 3, 4)
ADJ_CORNERS = (0, 1)


def place_in_grid():
    gx, gy = lax.axis_index("gx"), lax.axis_index("gy")
    return gx, gy, lax.axis_size("gx"), lax.axis_size("gy")


def lane_of(shape):
    return lax.broadcasted_iota(jnp.int32, shape, len(shape) - 1)


def row_of(shape):
    return lax.broadcasted_iota(jnp.int32, shape, len(shape) - 2)


def roll(value, by):
    by %= LANES
    return value if by == 0 else pltpu.roll(value, by, value.ndim - 1)


def weighted(shift, plus):
    total = None
    for k in range(1, REACH + 1):
        first = k if plus else k - 1
        term = coeffs[k - 1] * (shift(first) - shift(first + 1 - 2 * k))
        total = term if total is None else total + term
    return total


def with_x_halo(buf, field, d=0):
    own = buf[field, :, BASE + d : END + d, :]
    after = buf[field, :, END + d : END + d + SUB, :]
    before = buf[field, :, BASE - SUB + d : BASE + d, :]
    halo = jnp.where(row_of(after.shape) < REACH, after, before)
    return jnp.concatenate([own, halo], axis=1)


def diff_x(buf, field, plus, wide):
    if wide:
        return weighted(lambda d: with_x_halo(buf, field, d), plus)
    return weighted(lambda d: buf[field, :, BASE + d : END + d, :], plus)


def diff_y(field, halo, plus):
    lane = lane_of(field.shape)

    def shift(d):
        if d == 0:
            return field
        return roll(jnp.where(lane < d if d > 0 else lane >= LANES + d, halo, field), -d)

    return weighted(shift, plus)


def diff_z(field, plus):
    out = []
    for i in range(LAYERS):
        total = None
        for k in range(1, REACH + 1):
            first = i + (k if plus else k - 1)
            second = first + 1 - 2 * k
            has_first, has_second = 0 <= first < LAYERS, 0 <= second < LAYERS
            if has_first and has_second:
                term = coeffs[k - 1] * (field[first] - field[second])
            elif has_first:
                term = coeffs[k - 1] * field[first]
            elif has_second:
                term = -coeffs[k - 1] * field[second]
            else:
                continue
            total = term if total is None else total + term
        out.append(total)
    return jnp.stack(out)


def strip_x(buf, field, plus):
    return weighted(lambda d: buf[field, BASE + d : END + d, :], plus)


def strip_y(field, plus):
    return weighted(lambda d: roll(field, -d), plus)


def strip_z(field, plus):
    layer = lane_of(field.shape) // 32
    weights = {}
    for k in range(1, REACH + 1):
        first = k if plus else k - 1
        weights[first] = weights.get(first, 0.0) + coeffs[k - 1]
        weights[first + 1 - 2 * k] = weights.get(first + 1 - 2 * k, 0.0) - coeffs[k - 1]
    total = None
    for d, weight in weights.items():
        if abs(d) >= LAYERS:
            continue
        inside = (layer + d >= 0) & (layer + d < LAYERS)
        term = jnp.where(inside, weight, 0.0) * roll(field, -32 * d)
        total = term if total is None else total + term
    return total


def pack_edge(field):
    group = lane_of((SUB, LANES)) // 16
    packed = None
    for z in range(LAYERS):
        for tile in range(2):
            at = 2 * z + tile
            piece = roll(field[z, SUB * tile : SUB * (tile + 1)], 8 + 16 * at)
            packed = piece if packed is None else jnp.where(group == at, piece, packed)
    return packed


def pack_corners(edges, out_ref, slot):
    group = lane_of((SUB, LANES)) // 8 % 4
    top = row_of((SUB, LANES)) < REACH
    for start in range(0, len(edges), 4):
        packed = None
        for g, edge in enumerate(edges[start : start + 4]):
            piece = jnp.where(top, roll(edge, 8 * g - 4), roll(edge, 8 * g - 20))
            packed = piece if packed is None else jnp.where(group == g, piece, packed)
        out_ref[slot, start // 4] = packed


def strip_of(edge, low, high):
    half = lane_of(edge.shape) % 16 < 8
    first, last = jnp.where(half, low, edge), jnp.where(half, edge, high)
    side = lane_of(edge.shape) % 32 < 16
    tiles = [jnp.where(side, first, roll(last, 16)), jnp.where(side, roll(first, -16), last)]
    return jnp.concatenate(tiles, axis=0)


def y_halo_of_edges(low, high):
    merged = jnp.where(lane_of(low.shape) % 16 < 8, low, high)
    return jnp.stack([
        jnp.concatenate([roll(merged, 120 - 32 * z - 16 * tile) for tile in range(2)], axis=0)
        for z in range(LAYERS)
    ])


def y_halo_of_strip(strip):
    merged = jnp.where(lane_of(strip.shape) % 16 < 8, strip, roll(strip, -16))
    return jnp.stack([roll(merged, 120 - 32 * z) for z in range(LAYERS)])


def y_halo_of_corners(corner, g):
    return jnp.stack([roll(corner, 124 - 32 * z - 8 * g) for z in range(LAYERS)])


def strip_rows_of_corners(corner, g):
    side = lane_of(corner.shape) % 32 < 16
    return jnp.where(side, roll(corner, 4 - 8 * g), roll(corner, 20 - 8 * g))


class Chain:
    def __init__(self, refs, deep, shallow, edges, corners):
        (self.buf, self.edge, self.side, self.corner, self.corners_in,
         self.strips, self.send_sem, self.recv_sem) = refs
        self.deep, self.shallow = deep, shallow
        self.edges, self.corner_places = edges, corners

    def copies(self, slot):
        gx, gy, nx, ny = place_in_grid()
        out = []

        def add(dx, dy, src, dst):
            def inside(sx, sy):
                conds = []
                if sx:
                    conds.append(gx > 0 if sx < 0 else gx < nx - 1)
                if sy:
                    conds.append(gy > 0 if sy < 0 else gy < ny - 1)
                return conds[0] if len(conds) == 1 else jnp.logical_and(*conds)

            copy = pltpu.make_async_remote_copy(
                src_ref=src,
                dst_ref=dst,
                send_sem=self.send_sem.at[slot, len(out)],
                recv_sem=self.recv_sem.at[slot, len(out)],
                device_id=(lax.rem(gx + dx + nx, nx), lax.rem(gy + dy + ny, ny)),
                device_id_type=MESH,
            )
            out.append((inside(dx, dy), inside(-dx, -dy), copy))

        for dx in (-1, 1):
            for dy in (-1, 1):
                at = (1 - dx) // 2 * 2 + (1 - dy) // 2
                add(dx, dy, self.corner.at[slot], self.corners_in.at[slot, at])
        for dy in (-1, 1):
            add(0, dy, self.edge.at[slot], self.side.at[slot, (1 - dy) // 2])
        for fields, count in ((self.deep, SUB), (self.shallow, REACH)):
            for dx in (-1, 1):
                src = BASE if dx < 0 else END - count
                dst = END if dx < 0 else BASE - count
                part = pl.ds(fields[0], len(fields))
                add(dx, 0, self.buf.at[slot, part, :, pl.ds(src, count), :],
                    self.buf.at[slot, part, :, pl.ds(dst, count), :])
        return out

    def clear(self):
        for slot in range(2):
            for fields, count in ((self.deep, SUB), (self.shallow, REACH)):
                zero = jnp.zeros((len(fields), LAYERS, count, LANES), jnp.float32)
                part = pl.ds(fields[0], len(fields))
                self.buf[slot, part, :, BASE - count : BASE, :] = zero
                self.buf[slot, part, :, END : END + count, :] = zero
        self.side[...] = jnp.zeros_like(self.side)
        self.corners_in[...] = jnp.zeros_like(self.corners_in)

    def send(self, slot):
        edges = {}
        for i, place in enumerate(self.edges):
            edges[place] = pack_edge(self.own(slot, place))
            self.edge[slot, i] = edges[place]
        pack_corners([edges[place] for place in self.corner_places], self.corner, slot)
        for goes, _, copy in self.copies(slot):
            pl.when(goes)(copy.start)

    def wait_recv(self, slot):
        for _, arrives, copy in self.copies(slot):
            pl.when(arrives)(copy.wait_recv)

    def wait_send(self, slot):
        for goes, _, copy in self.copies(slot):
            pl.when(goes)(copy.wait_send)

    def own(self, slot, place):
        return self.buf[slot, place, :, BASE:END, :]

    def put(self, slot, place, value):
        self.buf[slot, place, :, BASE:END, :] = value

    def strip(self, slot, place):
        i = self.edges.index(place)
        return strip_of(self.edge[slot, i], self.side[slot, 0, i], self.side[slot, 1, i])

    def y_halo(self, slot, place):
        i = self.edges.index(place)
        return y_halo_of_edges(self.side[slot, 0, i], self.side[slot, 1, i])

    def corner_tiles(self, slot):
        shape = (SUB, LANES)
        first, top = lane_of(shape) % 8 < 4, row_of(shape) < REACH
        out = []
        for i in range(self.corner.shape[1]):
            here = [self.corners_in[slot, at, i] for at in range(4)]
            out.append(jnp.where(top, jnp.where(first, here[2], here[3]),
                                 jnp.where(first, here[0], here[1])))
        return out

    def wide_y_halo(self, slot, place, tiles):
        at = self.corner_places.index(place)
        corner = y_halo_of_corners(tiles[at // 4], at % 4)
        return jnp.concatenate([self.y_halo(slot, place), corner], axis=1)

    def set_strip_rows(self, place, strip, tiles):
        at = self.corner_places.index(place)
        rows = strip_rows_of_corners(tiles[at // 4], at % 4)
        self.strips[place, BASE:END, :] = strip
        self.strips[place, BASE - SUB : BASE, :] = rows
        self.strips[place, END : END + SUB, :] = rows


def put_wide(work, place, value):
    work[place, :, BASE:END, :] = value[:, :ROWS]
    work[place, :, END : END + REACH, :] = value[:, ROWS : ROWS + REACH]
    work[place, :, BASE - REACH : BASE, :] = value[:, ROWS + REACH :]


def log2(n):
    assert n > 0 and n & (n - 1) == 0
    return n.bit_length() - 1


def spread(traces_ref, row, lane, rows, store):
    steps, count = traces_ref.shape
    row_hit = lax.broadcasted_iota(jnp.int32, (rows, count), 0) == row
    lane_hit = lax.broadcasted_iota(jnp.int32, (LANES, count), 0) == lane
    lanes = jnp.where(lane_hit, 1.0, 0.0).astype(jnp.bfloat16)
    for t in range(steps):
        rest = traces_ref[t : t + 1, :]
        total = None
        for _ in range(3):
            piece = rest.astype(jnp.bfloat16).astype(jnp.float32)
            rest = rest - piece
            left = jnp.where(row_hit, piece, 0.0).astype(jnp.bfloat16)
            part = lax.dot_general(
                left, lanes, (((1,), (1,)), ((), ())), preferred_element_type=jnp.float32
            )
            total = part if total is None else total + part
        store(t, step_dt * total)


def positions(cells_ref, nx_cells, ny_cells):
    gx, gy, _, _ = place_in_grid()
    cells = cells_ref[...]
    layer = lax.shift_right_logical(cells, jnp.int32(log2(nx_cells * ny_cells)))
    at_x = lax.shift_right_logical(cells, jnp.int32(log2(ny_cells))) & (nx_cells - 1)
    return layer, at_x - gx * ROWS, (cells & (ny_cells - 1)) - gy * LANES


def kernel(
    dims,
    fwd_hbm, adj_hbm, labels_hbm, table_hbm, src_hbm, wav_hbm, rec_hbm, res_hbm,
    out_ref, gl_ref, gm_ref,
    table_ref, src_ref, wav_ref, rec_ref, res_ref,
    f_buf, f_edge, f_side, f_corner, f_corners_in, f_strips,
    a_buf, a_edge, a_side, a_corner, a_corners_in, a_strips,
    f_work, a_work, labels, lab, lab_edge, lab_side, mats, mats_s,
    inj_f, inj_s, inj_a, e_all, f_all, grads,
    in_sem, out_sem, f_send, f_recv, a_send, a_recv, l_send, l_recv,
):
    nx_cells, ny_cells = dims
    gx, gy, nx, ny = place_in_grid()
    steps = wav_ref.shape[0]

    fwd = Chain((f_buf, f_edge, f_side, f_corner, f_corners_in, f_strips, f_send, f_recv),
                (0, 1, 2), (3, 4, 5, 6, 7, 8), FWD_EDGES, FWD_CORNERS)
    adj = Chain((a_buf, a_edge, a_side, a_corner, a_corners_in, a_strips, a_send, a_recv),
                (0, 1, 2), (3, 4, 5), ADJ_EDGES, ADJ_CORNERS)

    loads = []

    def load(src, dst):
        copy = pltpu.make_async_copy(src, dst, in_sem.at[len(loads)])
        copy.start()
        loads.append(copy)

    own_rows = pl.ds(BASE, ROWS)
    load(labels_hbm, labels)
    for place, number in enumerate(FWD):
        load(fwd_hbm.at[number], f_buf.at[0, place, :, own_rows, :])
    for place, number in enumerate(ADJ):
        load(adj_hbm.at[number], a_buf.at[0, place, :, own_rows, :])
    first = len(loads)
    for src, dst in (
        (table_hbm, table_ref), (src_hbm, src_ref), (wav_hbm, wav_ref),
        (rec_hbm, rec_ref), (res_hbm, res_ref),
    ):
        load(src, dst)

    fwd.clear()
    adj.clear()
    lab[...] = jnp.zeros_like(lab)
    lab_side[...] = jnp.zeros_like(lab_side)
    barrier = pltpu.get_barrier_semaphore()
    around = [(dx, dy) for dx in (-1, 0, 1) for dy in (-1, 0, 1) if dx or dy]
    for dx, dy in around:
        to = (lax.rem(gx + dx + nx, nx), lax.rem(gy + dy + ny, ny))
        pl.semaphore_signal(barrier, inc=1, device_id=to, device_id_type=MESH)

    loads[0].wait()
    lab[0, :, BASE:END, :] = labels[...].astype(jnp.float32)
    lab_edge[0] = pack_edge(lab[0, :, BASE:END, :])
    lab_copies = []
    for goes, arrives, src, dst, axis, to in (
        (gx > 0, gx < nx - 1, lab.at[0, :, pl.ds(BASE, REACH), :], lab.at[0, :, pl.ds(END, REACH), :], "gx", lax.rem(gx + nx - 1, nx)),
        (gx < nx - 1, gx > 0, lab.at[0, :, pl.ds(END - REACH, REACH), :], lab.at[0, :, pl.ds(BASE - REACH, REACH), :], "gx", lax.rem(gx + 1, nx)),
        (gy > 0, gy < ny - 1, lab_edge, lab_side.at[1], "gy", lax.rem(gy + ny - 1, ny)),
        (gy < ny - 1, gy > 0, lab_edge, lab_side.at[0], "gy", lax.rem(gy + 1, ny)),
    ):
        copy = pltpu.make_async_remote_copy(
            src_ref=src, dst_ref=dst, send_sem=l_send.at[len(lab_copies)],
            recv_sem=l_recv.at[len(lab_copies)], device_id={axis: to}, device_id_type=MESH,
        )
        lab_copies.append((goes, arrives, copy))

    for copy in loads[1:first]:
        copy.wait()
    pl.semaphore_wait(barrier, len(around))
    fwd.send(0)
    adj.send(0)
    for goes, _, copy in lab_copies:
        pl.when(goes)(copy.start)

    for copy in loads[first:]:
        copy.wait()
    layer, at_x, at_y = positions(src_ref, nx_cells, ny_cells)
    wide = ROWS + SUB
    here = jnp.where(at_x < 0, at_x + wide, at_x)
    row = jnp.where((at_x >= -REACH) & (at_x < ROWS + REACH), layer * wide + here, -1)

    def store_wide(t, value):
        inj_f[t] = value.reshape(LAYERS, wide, LANES)

    spread(wav_ref, row, at_y, LAYERS * wide, store_wide)
    column = jnp.where((at_y >= -REACH) & (at_y < 0), 32 * layer + 8 + at_y, -1)
    column = jnp.where((at_y >= LANES) & (at_y < LANES + REACH), 32 * layer + 24 + at_y - LANES, column)

    def store_strip(t, value):
        inj_s[t] = value

    spread(wav_ref, at_x, column, ROWS, store_strip)
    layer, at_x, at_y = positions(rec_ref, nx_cells, ny_cells)
    row = jnp.where((at_x >= 0) & (at_x < ROWS), layer * ROWS + at_x, -1)

    def store_own(t, value):
        inj_a[t] = value.reshape(LAYERS, ROWS, LANES)

    spread(res_ref, row, at_y, LAYERS * ROWS, store_own)

    for _, arrives, copy in lab_copies:
        pl.when(arrives)(copy.wait_recv)

    def materials(label, inside, out):
        for prop in range(3):
            value = jnp.full(label.shape, table_ref[prop, 0])
            for phase in range(1, table_ref.shape[1]):
                value = jnp.where(label == phase, table_ref[prop, phase], value)
            value = step_dt * value if prop < 2 else step_dt / value
            out[prop] = jnp.where(inside, value, 0.0)

    shape = (LAYERS, wide, LANES)
    r = row_of(shape)
    inside = (r < ROWS) | ((r < ROWS + REACH) & (gx < nx - 1)) | ((r >= ROWS + REACH) & (gx > 0))
    materials(with_x_halo(lab, 0), inside, mats)
    lane = lane_of((ROWS, LANES))
    column = lane % 16 + jnp.where(lane % 32 < 16, -8, LANES - 8)
    inside = ((column >= 0) | (gy > 0)) & ((column < LANES) | (gy < ny - 1))
    materials(strip_of(lab_edge[0], lab_side[0, 0], lab_side[1, 0]), inside, mats_s)

    def forward_step(t):
        slot = t % 2
        other = 1 - slot
        buf = f_buf.at[slot]
        fwd.wait_recv(slot)
        tiles = fwd.corner_tiles(slot)
        div = []
        sxx, sxy, sxz, syy, syz, szz, vx, vy, vz = range(9)
        for first, second, third, plus in (
            (sxx, sxy, sxz, 0), (sxy, syy, syz, 1), (sxz, syz, szz, 2)
        ):
            div.append(
                diff_x(buf, first, plus == 0, True)
                + diff_y(with_x_halo(buf, second), fwd.wide_y_halo(slot, second, tiles), plus == 1)
                + diff_z(with_x_halo(buf, third), plus == 2)
            )
        strips = [fwd.strip(slot, place) for place in range(9)]
        for place in (sxx, sxy, sxz):
            fwd.set_strip_rows(place, strips[place], tiles)
        strip_div = [
            strip_x(f_strips, sxx, True) + strip_y(strips[sxy], False) + strip_z(strips[sxz], False),
            strip_x(f_strips, sxy, False) + strip_y(strips[syy], True) + strip_z(strips[syz], False),
            strip_x(f_strips, sxz, False) + strip_y(strips[syz], False) + strip_z(strips[szz], True),
        ]
        if t > 0:
            fwd.wait_send(other)
        halos = []
        for i in range(3):
            new = with_x_halo(buf, vx + i) + mats[2] * div[i]
            side = strips[vx + i] + mats_s[2] * strip_div[i]
            if i == 2:
                new, side = new + inj_f[t], side + inj_s[t]
            put_wide(f_work, i, new)
            fwd.put(other, vx + i, new[:, :ROWS])
            halos.append(y_halo_of_strip(side))
        v = [fwd.own(other, vx + i) for i in range(3)]
        strain = (
            diff_x(f_work, 0, False, False),
            diff_y(v[1], halos[1], False),
            diff_z(v[2], False),
            diff_y(v[0], halos[0], True) + diff_x(f_work, 1, True, False),
            diff_z(v[0], True) + diff_x(f_work, 2, True, False),
            diff_z(v[1], True) + diff_y(v[2], halos[2], True),
        )
        for i in range(6):
            e_all[t, i] = strain[i]

        if t < steps - 1:
            lam, shear = mats[0, :, :ROWS], mats[1, :, :ROWS]
            exx, eyy, ezz, exy, exz, eyz = strain
            base, twice = lam * (exx + eyy + ezz), 2.0 * shear
            for place, inc in (
                (sxx, base + twice * exx), (sxy, shear * exy), (sxz, shear * exz),
                (syy, base + twice * eyy), (syz, shear * eyz), (szz, base + twice * ezz),
            ):
                fwd.put(other, place, fwd.own(slot, place) + inc)
            fwd.send(other)

    def adjoint_step(t):
        slot = t % 2
        other = 1 - slot
        buf = a_buf.at[slot]
        adj.wait_recv(slot)
        tiles = adj.corner_tiles(slot)
        vx, vy, vz, sxx, sxy, sxz, syy, syz, szz = range(9)
        u = [with_x_halo(buf, i) for i in range(3)]
        u_halo = [adj.wide_y_halo(slot, i, tiles) for i in range(2)]
        u_own = adj.own(slot, vz)
        exx, eyy, ezz = diff_x(buf, vx, False, True), diff_y(u[1], u_halo[1], False), diff_z(u[2], False)
        exy = diff_y(u[0], u_halo[0], True) + diff_x(buf, vy, True, True)
        exz = diff_z(u[0], True) + diff_x(buf, vz, True, True)
        eyz = diff_z(adj.own(slot, vy), True) + diff_y(u_own, adj.y_halo(slot, vz), True)
        for i, value in enumerate((exx, eyy, ezz, exy, exz)):
            f_all[t, i] = value[:, :ROWS]
        f_all[t, 5] = eyz
        side = [adj.strip(slot, i) for i in range(3)]
        for i in range(2):
            adj.set_strip_rows(i, side[i], tiles)
        side_xx, side_yy, side_zz = strip_x(a_strips, vx, False), strip_y(side[1], False), strip_z(side[2], False)
        side_xy = strip_y(side[0], True) + strip_x(a_strips, vy, True)
        side_yz = strip_z(side[1], True) + strip_y(side[2], True)
        if t > 0:
            adj.wait_send(other)
        lam, shear = mats[0], mats[1]
        base = lam * (exx + eyy + ezz)
        for i, (place, inc) in enumerate(
            ((sxx, base + 2.0 * shear * exx), (sxy, shear * exy), (sxz, shear * exz))
        ):
            new = with_x_halo(buf, place) - inc
            put_wide(a_work, i, new)
            adj.put(other, place, new[:, :ROWS])
        base, shear = base[:, :ROWS], shear[:, :ROWS]
        for place, inc in (
            (syy, base + 2.0 * shear * eyy[:, :ROWS]),
            (syz, shear * eyz),
            (szz, base + 2.0 * shear * ezz[:, :ROWS]),
        ):
            adj.put(other, place, adj.own(slot, place) - inc)
        lam, shear = mats_s[0], mats_s[1]
        side_inc = {
            sxy: shear * side_xy,
            syy: lam * (side_xx + side_yy + side_zz) + 2.0 * shear * side_yy,
            syz: shear * side_yz,
        }
        halo = {
            place: y_halo_of_strip(adj.strip(slot, place) - inc) for place, inc in side_inc.items()
        }
        new = {place: adj.own(other, place) for place in (sxy, sxz, syy, syz, szz)}
        div = (
            diff_x(a_work, 0, True, False) + diff_y(new[sxy], halo[sxy], False) + diff_z(new[sxz], False),
            diff_x(a_work, 1, False, False) + diff_y(new[syy], halo[syy], True) + diff_z(new[syz], False),
            diff_x(a_work, 2, False, False) + diff_y(new[syz], halo[syz], False) + diff_z(new[szz], True),
        )
        buoy = mats[2, :, :ROWS]
        for i in range(3):
            value = adj.own(slot, i) - buoy * div[i]
            adj.put(other, i, value + inj_a[t] if i == 2 else value)
        if t < steps - 1:
            adj.send(other)

    for t in range(steps):
        forward_step(t)
        adjoint_step(t)

    last = (steps - 1) % 2
    fwd.wait_send(last)
    adj.wait_send(last)
    for goes, _, copy in lab_copies:
        pl.when(goes)(copy.wait_send)

    for place, number in enumerate(ADJ):
        out_ref[number] = adj.own(1 - last, place)

    grad_l = grad_m = None
    for t in range(steps):
        e = [e_all[steps - 1 - t, i] for i in range(6)]
        f = [f_all[t, i] for i in range(6)]
        more_l = (e[0] + e[1] + e[2]) * (f[0] + f[1] + f[2])
        more_m = 2.0 * (e[0] * f[0] + e[1] * f[1] + e[2] * f[2])
        more_m = more_m + e[3] * f[3] + e[4] * f[4] + e[5] * f[5]
        grad_l = more_l if grad_l is None else grad_l + more_l
        grad_m = more_m if grad_m is None else grad_m + more_m
    gl_ref[...] = step_dt * grad_l
    gm_ref[...] = step_dt * grad_m


def hand_over(*refs):
    sem = refs[-1]
    copies = [pltpu.make_async_copy(refs[i], refs[3 + i], sem.at[i]) for i in range(3)]
    for copy in copies:
        copy.start()
    for copy in copies:
        copy.wait()


def shards(fwd, adj, labels, table, src, wav, rec, res):
    assert labels.shape == (LAYERS, ROWS, LANES)
    dims = (ROWS * lax.axis_size("gx"), LANES * lax.axis_size("gy"))
    steps = wav.shape[0]
    f32 = jnp.float32
    block, tile = (LAYERS, ROWS, LANES), (SUB, LANES)
    wide = (LAYERS, ROWS + SUB, LANES)

    def vmem(*shape):
        return pltpu.VMEM(shape, f32)

    def chain(edges, corners, strips):
        return [
            vmem(2, 9, LAYERS, PADDED, LANES),
            vmem(2, edges, *tile),
            vmem(2, 2, edges, *tile),
            vmem(2, corners, *tile),
            vmem(2, 4, corners, *tile),
            vmem(strips, PADDED, LANES),
        ]

    in_hbm = pl.BlockSpec(memory_space=pl.ANY)
    in_vmem = pl.BlockSpec(memory_space=pltpu.VMEM)
    dma = pltpu.SemaphoreType.DMA
    operands = [
        pltpu.with_memory_space_constraint(x, pltpu.HBM)
        for x in (fwd, adj, labels, table, src.reshape(1, -1), wav, rec.reshape(1, -1), res)
    ]
    results = pl.pallas_call(
        functools.partial(kernel, dims),
        out_shape=(
            pltpu.VMEM(fwd.shape, f32),
            pltpu.VMEM(block, f32),
            pltpu.VMEM(block, f32),
        ),
        in_specs=[in_hbm] * 8,
        out_specs=(in_vmem, in_vmem, in_vmem),
        scratch_shapes=[
            pltpu.SMEM(table.shape, f32),
            pltpu.VMEM((1,) + src.shape, jnp.int32),
            vmem(*wav.shape),
            pltpu.VMEM((1,) + rec.shape, jnp.int32),
            vmem(*res.shape),
        ] + chain(9, 2, 3) + chain(6, 1, 2) + [
            vmem(3, LAYERS, PADDED, LANES),
            vmem(3, LAYERS, PADDED, LANES),
            pltpu.VMEM(block, jnp.int32),
            vmem(1, LAYERS, PADDED, LANES),
            vmem(1, *tile),
            vmem(2, 1, *tile),
            vmem(3, *wide),
            vmem(3, ROWS, LANES),
            vmem(steps, *wide),
            vmem(steps, ROWS, LANES),
            vmem(steps, *block),
            vmem(steps, 6, *block),
            vmem(steps, 6, *block),
            vmem(2, *block),
            dma((24,)), dma((11,)),
            dma((2, 10)), dma((2, 10)), dma((2, 10)), dma((2, 10)),
            dma((4,)), dma((4,)),
        ],
        compiler_params=pltpu.CompilerParams(
            collective_id=0, has_side_effects=True, vmem_limit_bytes=40 * 1024 * 1024
        ),
    )(*operands)
    return pl.pallas_call(
        hand_over,
        out_shape=(
            pltpu.HBM(fwd.shape, f32),
            pltpu.HBM(block, f32),
            pltpu.HBM(block, f32),
        ),
        in_specs=[in_hbm] * 3,
        out_specs=(in_hbm,) * 3,
        scratch_shapes=[dma((3,))],
    )(*(pltpu.with_memory_space_constraint(r, pltpu.VMEM) for r in results))


def solution(mesh):
    state, cells = P(None, None, "gx", "gy"), P(None, "gx", "gy")
    return jax.shard_map(
        shards,
        mesh=mesh,
        in_specs=(state, state, cells, P(), P(), P(), P(), P()),
        out_specs=(state, cells, cells),
        check_vma=False,
    )
```

```python
import functools

import jax
import jax.numpy as jnp
from jax import lax
from jax.experimental import pallas as pl
from jax.experimental.pallas import tpu as pltpu
from jax.sharding import PartitionSpec as P

coeffs = (1225.0 / 1024.0, -245.0 / 3072.0, 49.0 / 5120.0, -5.0 / 7168.0)
step_dt = 0.1
MESH = pl.DeviceIdType.MESH

LAYERS, ROWS, LANES, SUB = 4, 16, 128, 8
REACH = 4
BASE = 16
PADDED = ROWS + 2 * BASE
END = BASE + ROWS

FWD = (3, 6, 7, 4, 8, 5, 0, 1, 2)
ADJ = (0, 1, 2, 3, 6, 7, 4, 8, 5)
FWD_EDGES = tuple(range(9))
ADJ_EDGES = (0, 1, 2, 4, 6, 7)
FWD_CORNERS = (0, 1, 2, 3, 4)
ADJ_CORNERS = (0, 1)


def place_in_grid():
    gx, gy = lax.axis_index("gx"), lax.axis_index("gy")
    return gx, gy, lax.axis_size("gx"), lax.axis_size("gy")


def lane_of(shape):
    return lax.broadcasted_iota(jnp.int32, shape, len(shape) - 1)


def row_of(shape):
    return lax.broadcasted_iota(jnp.int32, shape, len(shape) - 2)


def roll(value, by):
    by %= LANES
    return value if by == 0 else pltpu.roll(value, by, value.ndim - 1)


def weighted(shift, plus):
    total = None
    for k in range(1, REACH + 1):
        first = k if plus else k - 1
        term = coeffs[k - 1] * (shift(first) - shift(first + 1 - 2 * k))
        total = term if total is None else total + term
    return total


def halo_rows(buf, field, d=0):
    after = buf[field, :, END + d : END + d + SUB, :]
    before = buf[field, :, BASE - SUB + d : BASE + d, :]
    return jnp.where(row_of(after.shape) < REACH, after, before)


def halo_diff_x(buf, field, plus):
    return weighted(lambda d: halo_rows(buf, field, d), plus)


def diff_x(buf, field, plus):
    return weighted(lambda d: buf[field, :, BASE + d : END + d, :], plus)


def diff_y(field, halo, plus):
    lane = lane_of(field.shape)

    def shift(d):
        if d == 0:
            return field
        return roll(jnp.where(lane < d if d > 0 else lane >= LANES + d, halo, field), -d)

    return weighted(shift, plus)


def near_and_far(shift, plus):
    sign = -1 if plus else 1
    taps = [shift(sign * k) for k in range(REACH)]
    near = far = None
    for k in range(REACH):
        one, two = coeffs[k] * taps[k], coeffs[REACH - 1 - k] * taps[k]
        near = one if near is None else near + one
        far = two if far is None else far + two
    return near, far


def ring_diff_y(field, plus):
    near, far = near_and_far(lambda d: roll(field, -d), plus)
    return roll(far, -REACH) - near if plus else near - roll(far, REACH)


def diff_z(field, plus):
    out = []
    for i in range(LAYERS):
        total = None
        for k in range(1, REACH + 1):
            first = i + (k if plus else k - 1)
            second = first + 1 - 2 * k
            has_first, has_second = 0 <= first < LAYERS, 0 <= second < LAYERS
            if has_first and has_second:
                term = coeffs[k - 1] * (field[first] - field[second])
            elif has_first:
                term = coeffs[k - 1] * field[first]
            elif has_second:
                term = -coeffs[k - 1] * field[second]
            else:
                continue
            total = term if total is None else total + term
        out.append(total)
    return jnp.stack(out)


def strip_x(buf, field, plus):
    return weighted(lambda d: buf[field, BASE + d : END + d, :], plus)


strip_y = ring_diff_y


def strip_z(field, plus):
    layer = lane_of(field.shape) // 32
    weights = {}
    for k in range(1, REACH + 1):
        first = k if plus else k - 1
        weights[first] = weights.get(first, 0.0) + coeffs[k - 1]
        weights[first + 1 - 2 * k] = weights.get(first + 1 - 2 * k, 0.0) - coeffs[k - 1]
    total = None
    for d, weight in weights.items():
        if abs(d) >= LAYERS:
            continue
        inside = (layer + d >= 0) & (layer + d < LAYERS)
        term = jnp.where(inside, weight, 0.0) * roll(field, -32 * d)
        total = term if total is None else total + term
    return total


def pack_edge(field):
    group = lane_of((SUB, LANES)) // 16
    packed = None
    for z in range(LAYERS):
        for tile in range(2):
            at = 2 * z + tile
            piece = roll(field[z, SUB * tile : SUB * (tile + 1)], 8 + 16 * at)
            packed = piece if packed is None else jnp.where(group == at, piece, packed)
    return packed


def pack_corners(edges, out_ref, slot):
    group = lane_of((SUB, LANES)) // 8 % 4
    top = row_of((SUB, LANES)) < REACH
    for start in range(0, len(edges), 4):
        packed = None
        for g, edge in enumerate(edges[start : start + 4]):
            piece = jnp.where(top, roll(edge, 8 * g - 4), roll(edge, 8 * g - 20))
            packed = piece if packed is None else jnp.where(group == g, piece, packed)
        out_ref[slot, start // 4] = packed


def strip_of(edge, low, high):
    half = lane_of(edge.shape) % 16 < 8
    first, last = jnp.where(half, low, edge), jnp.where(half, edge, high)
    side = lane_of(edge.shape) % 32 < 16
    tiles = [jnp.where(side, first, roll(last, 16)), jnp.where(side, roll(first, -16), last)]
    return jnp.concatenate(tiles, axis=0)


def end_terms(lack, plus):
    p = lane_of(lack.shape) % 16
    before, after = jnp.where(p < 8, lack, 0.0), jnp.where(p < 8, 0.0, lack)
    first_lanes = last_lanes = None
    for k in range(1, REACH + 1):
        first = k if plus else k - 1
        second = first + 1 - 2 * k
        if first > 0:
            term = coeffs[k - 1] * roll(after, -first)
            last_lanes = term if last_lanes is None else last_lanes + term
        if second < 0:
            term = coeffs[k - 1] * roll(before, -second)
            first_lanes = -term if first_lanes is None else first_lanes - term
    return jnp.where(p < 8, last_lanes, first_lanes)


def at_ends(value):
    lane = lane_of(value.shape)
    return jnp.where((lane < REACH) | (lane >= LANES - REACH), value, 0.0)


def ring_correction(edge, low, high, plus):
    total = end_terms(jnp.where(lane_of(edge.shape) % 16 < 8, low, high) - edge, plus)
    return jnp.stack([
        jnp.concatenate([at_ends(roll(total, 120 - 32 * z - 16 * t)) for t in range(2)], axis=0)
        for z in range(LAYERS)
    ])


def y_ends_of_strip(strip, plus):
    merged = jnp.where(lane_of(strip.shape) % 16 < 8, strip, roll(strip, -16))
    total = end_terms(merged, plus)
    return jnp.stack([at_ends(roll(total, 120 - 32 * z)) for z in range(LAYERS)])


def stencil_matrix(plus):
    source = lax.broadcasted_iota(jnp.int32, (LANES, LANES), 0)
    off = source - lane_of((LANES, LANES))
    total = jnp.zeros((LANES, LANES), jnp.float32)
    for k in range(1, REACH + 1):
        first = k if plus else k - 1
        total = jnp.where(off == first, coeffs[k - 1], total)
        total = jnp.where(off == first + 1 - 2 * k, -coeffs[k - 1], total)
    return total


def inner_diff_y(fields, matrix):
    rows = LAYERS * ROWS
    stacked = jnp.concatenate([f.reshape(rows, LANES) for f in fields], axis=0)
    out = jnp.dot(
        stacked, matrix, precision=lax.Precision.HIGHEST, preferred_element_type=jnp.float32
    )
    return [
        out[i * rows : (i + 1) * rows].reshape(LAYERS, ROWS, LANES) for i in range(len(fields))
    ]


def y_halo_of_corners(corner, g):
    return jnp.stack([roll(corner, 124 - 32 * z - 8 * g) for z in range(LAYERS)])


def strip_rows_of_corners(corner, g):
    side = lane_of(corner.shape) % 32 < 16
    return jnp.where(side, roll(corner, 4 - 8 * g), roll(corner, 20 - 8 * g))


class Chain:
    def __init__(self, refs, deep, shallow, edges, corners):
        (self.buf, self.edge, self.side, self.corner, self.corners_in,
         self.strips, self.send_sem, self.recv_sem) = refs
        self.deep, self.shallow = deep, shallow
        self.edges, self.corner_places = edges, corners

    def copies(self, slot):
        gx, gy, nx, ny = place_in_grid()
        out = []

        def add(dx, dy, src, dst):
            def inside(sx, sy):
                conds = []
                if sx:
                    conds.append(gx > 0 if sx < 0 else gx < nx - 1)
                if sy:
                    conds.append(gy > 0 if sy < 0 else gy < ny - 1)
                return conds[0] if len(conds) == 1 else jnp.logical_and(*conds)

            copy = pltpu.make_async_remote_copy(
                src_ref=src,
                dst_ref=dst,
                send_sem=self.send_sem.at[slot, len(out)],
                recv_sem=self.recv_sem.at[slot, len(out)],
                device_id=(lax.rem(gx + dx + nx, nx), lax.rem(gy + dy + ny, ny)),
                device_id_type=MESH,
            )
            out.append((inside(dx, dy), inside(-dx, -dy), copy))

        for dx in (-1, 1):
            for dy in (-1, 1):
                at = (1 - dx) // 2 * 2 + (1 - dy) // 2
                add(dx, dy, self.corner.at[slot], self.corners_in.at[slot, at])
        for dy in (-1, 1):
            add(0, dy, self.edge.at[slot], self.side.at[slot, (1 - dy) // 2])
        for fields, count in ((self.deep, SUB), (self.shallow, REACH)):
            for dx in (-1, 1):
                src = BASE if dx < 0 else END - count
                dst = END if dx < 0 else BASE - count
                part = pl.ds(fields[0], len(fields))
                add(dx, 0, self.buf.at[slot, part, :, pl.ds(src, count), :],
                    self.buf.at[slot, part, :, pl.ds(dst, count), :])
        return out

    def clear(self):
        for slot in range(2):
            for fields, count in ((self.deep, SUB), (self.shallow, REACH)):
                zero = jnp.zeros((len(fields), LAYERS, count, LANES), jnp.float32)
                part = pl.ds(fields[0], len(fields))
                self.buf[slot, part, :, BASE - count : BASE, :] = zero
                self.buf[slot, part, :, END : END + count, :] = zero
        self.side[...] = jnp.zeros_like(self.side)
        self.corners_in[...] = jnp.zeros_like(self.corners_in)

    def pack(self, slot):
        edges = []
        for place in self.corner_places:
            edges.append(pack_edge(self.own(slot, place)))
            self.edge[slot, self.edges.index(place)] = edges[-1]
        pack_corners(edges, self.corner, slot)

    def pack_rest(self, slot):
        for i, place in enumerate(self.edges):
            if place not in self.corner_places:
                self.edge[slot, i] = pack_edge(self.own(slot, place))

    def start(self, slot, first, last):
        for goes, _, copy in self.copies(slot)[first:last]:
            pl.when(goes)(copy.start)

    def send(self, slot):
        self.pack(slot)
        self.start(slot, 0, 4)
        self.start(slot, 6, 10)
        self.pack_rest(slot)
        self.start(slot, 4, 6)

    def wait_recv(self, slot):
        for _, arrives, copy in self.copies(slot):
            pl.when(arrives)(copy.wait_recv)

    def wait_send(self, slot):
        for goes, _, copy in self.copies(slot):
            pl.when(goes)(copy.wait_send)

    def own(self, slot, place):
        return self.buf[slot, place, :, BASE:END, :]

    def put(self, slot, place, value):
        self.buf[slot, place, :, BASE:END, :] = value

    def strip(self, slot, place):
        i = self.edges.index(place)
        return strip_of(self.edge[slot, i], self.side[slot, 0, i], self.side[slot, 1, i])

    def ring_correction(self, slot, place, plus):
        i = self.edges.index(place)
        return ring_correction(
            self.edge[slot, i], self.side[slot, 0, i], self.side[slot, 1, i], plus
        )

    def corner_tiles(self, slot):
        shape = (SUB, LANES)
        first, top = lane_of(shape) % 8 < 4, row_of(shape) < REACH
        out = []
        for i in range(self.corner.shape[1]):
            here = [self.corners_in[slot, at, i] for at in range(4)]
            out.append(jnp.where(top, jnp.where(first, here[2], here[3]),
                                 jnp.where(first, here[0], here[1])))
        return out

    def corner_y_halo(self, place, tiles):
        at = self.corner_places.index(place)
        return y_halo_of_corners(tiles[at // 4], at % 4)

    def set_strip_rows(self, place, strip, tiles):
        at = self.corner_places.index(place)
        rows = strip_rows_of_corners(tiles[at // 4], at % 4)
        self.strips[place, BASE:END, :] = strip
        self.strips[place, BASE - SUB : BASE, :] = rows
        self.strips[place, END : END + SUB, :] = rows


def put_halo_rows(work, place, value):
    work[place, :, END : END + REACH, :] = value[:, :REACH]
    work[place, :, BASE - REACH : BASE, :] = value[:, REACH:]


def log2(n):
    assert n > 0 and n & (n - 1) == 0
    return n.bit_length() - 1


def spread(traces_ref, row, lane, rows, store):
    steps, count = traces_ref.shape
    row_hit = lax.broadcasted_iota(jnp.int32, (rows, count), 0) == row
    lane_hit = lax.broadcasted_iota(jnp.int32, (LANES, count), 0) == lane
    lanes = jnp.where(lane_hit, 1.0, 0.0).astype(jnp.bfloat16)
    for t in range(steps):
        rest = traces_ref[t : t + 1, :]
        total = None
        for _ in range(3):
            piece = rest.astype(jnp.bfloat16).astype(jnp.float32)
            rest = rest - piece
            left = jnp.where(row_hit, piece, 0.0).astype(jnp.bfloat16)
            part = lax.dot_general(
                left, lanes, (((1,), (1,)), ((), ())), preferred_element_type=jnp.float32
            )
            total = part if total is None else total + part
        store(t, step_dt * total)


def positions(cells_ref, nx_cells, ny_cells):
    gx, gy, _, _ = place_in_grid()
    cells = cells_ref[...]
    layer = lax.shift_right_logical(cells, jnp.int32(log2(nx_cells * ny_cells)))
    at_x = lax.shift_right_logical(cells, jnp.int32(log2(ny_cells))) & (nx_cells - 1)
    return layer, at_x - gx * ROWS, (cells & (ny_cells - 1)) - gy * LANES


def kernel(
    dims,
    fwd_hbm, adj_hbm, labels_hbm, table_hbm, src_hbm, wav_hbm, rec_hbm, res_hbm,
    out_ref, gl_ref, gm_ref,
    table_ref, src_ref, wav_ref, rec_ref, res_ref,
    f_buf, f_edge, f_side, f_corner, f_corners_in, f_strips,
    a_buf, a_edge, a_side, a_corner, a_corners_in, a_strips,
    matrices, f_work, a_work, f_part, a_part, labels, lab, lab_edge, lab_side, mats, mats_s,
    inj_f, inj_s, inj_a, e_all, f_all, grads,
    in_sem, out_sem, f_send, f_recv, a_send, a_recv, l_send, l_recv,
):
    nx_cells, ny_cells = dims
    gx, gy, nx, ny = place_in_grid()
    steps = wav_ref.shape[0]

    fwd = Chain((f_buf, f_edge, f_side, f_corner, f_corners_in, f_strips, f_send, f_recv),
                (0, 1, 2), (3, 4, 5, 6, 7, 8), FWD_EDGES, FWD_CORNERS)
    adj = Chain((a_buf, a_edge, a_side, a_corner, a_corners_in, a_strips, a_send, a_recv),
                (0, 1, 2), (3, 4, 5), ADJ_EDGES, ADJ_CORNERS)

    loads = []

    def load(src, dst):
        copy = pltpu.make_async_copy(src, dst, in_sem.at[len(loads)])
        copy.start()
        loads.append(copy)

    own_rows = pl.ds(BASE, ROWS)
    load(labels_hbm, labels)
    for place, number in enumerate(FWD):
        load(fwd_hbm.at[number], f_buf.at[0, place, :, own_rows, :])
    for place, number in enumerate(ADJ):
        load(adj_hbm.at[number], a_buf.at[0, place, :, own_rows, :])
    first = len(loads)
    for src, dst in (
        (table_hbm, table_ref), (src_hbm, src_ref), (wav_hbm, wav_ref),
        (rec_hbm, rec_ref), (res_hbm, res_ref),
    ):
        load(src, dst)

    fwd.clear()
    adj.clear()
    lab[...] = jnp.zeros_like(lab)
    lab_side[...] = jnp.zeros_like(lab_side)
    barrier = pltpu.get_barrier_semaphore()
    around = [(dx, dy) for dx in (-1, 0, 1) for dy in (-1, 0, 1) if dx or dy]
    for dx, dy in around:
        to = (lax.rem(gx + dx + nx, nx), lax.rem(gy + dy + ny, ny))
        pl.semaphore_signal(barrier, inc=1, device_id=to, device_id_type=MESH)

    loads[0].wait()
    lab[0, :, BASE:END, :] = labels[...].astype(jnp.float32)
    lab_edge[0] = pack_edge(lab[0, :, BASE:END, :])
    lab_copies = []
    for goes, arrives, src, dst, axis, to in (
        (gx > 0, gx < nx - 1, lab.at[0, :, pl.ds(BASE, REACH), :], lab.at[0, :, pl.ds(END, REACH), :], "gx", lax.rem(gx + nx - 1, nx)),
        (gx < nx - 1, gx > 0, lab.at[0, :, pl.ds(END - REACH, REACH), :], lab.at[0, :, pl.ds(BASE - REACH, REACH), :], "gx", lax.rem(gx + 1, nx)),
        (gy > 0, gy < ny - 1, lab_edge, lab_side.at[1], "gy", lax.rem(gy + ny - 1, ny)),
        (gy < ny - 1, gy > 0, lab_edge, lab_side.at[0], "gy", lax.rem(gy + 1, ny)),
    ):
        copy = pltpu.make_async_remote_copy(
            src_ref=src, dst_ref=dst, send_sem=l_send.at[len(lab_copies)],
            recv_sem=l_recv.at[len(lab_copies)], device_id={axis: to}, device_id_type=MESH,
        )
        lab_copies.append((goes, arrives, copy))

    for copy in loads[1:first]:
        copy.wait()
    for chain in (fwd, adj):
        chain.pack(0)
        chain.pack_rest(0)
    pl.semaphore_wait(barrier, len(around))
    fwd.start(0, 0, 10)
    adj.start(0, 0, 10)
    for goes, _, copy in lab_copies:
        pl.when(goes)(copy.start)

    for copy in loads[first:]:
        copy.wait()
    layer, at_x, at_y = positions(src_ref, nx_cells, ny_cells)
    wide = ROWS + SUB
    here = jnp.where(at_x < 0, at_x + wide, at_x)
    row = jnp.where((at_x >= -REACH) & (at_x < ROWS + REACH), layer * wide + here, -1)

    def store_wide(t, value):
        inj_f[t] = value.reshape(LAYERS, wide, LANES)

    spread(wav_ref, row, at_y, LAYERS * wide, store_wide)
    column = jnp.where((at_y >= -REACH) & (at_y < 0), 32 * layer + 8 + at_y, -1)
    column = jnp.where((at_y >= LANES) & (at_y < LANES + REACH), 32 * layer + 24 + at_y - LANES, column)

    def store_strip(t, value):
        inj_s[t] = value

    spread(wav_ref, at_x, column, ROWS, store_strip)
    layer, at_x, at_y = positions(rec_ref, nx_cells, ny_cells)
    row = jnp.where((at_x >= 0) & (at_x < ROWS), layer * ROWS + at_x, -1)

    def store_own(t, value):
        inj_a[t] = value.reshape(LAYERS, ROWS, LANES)

    spread(res_ref, row, at_y, LAYERS * ROWS, store_own)

    matrices[0] = stencil_matrix(True)
    matrices[1] = stencil_matrix(False)

    for _, arrives, copy in lab_copies:
        pl.when(arrives)(copy.wait_recv)

    def materials(label, inside, out):
        for prop in range(3):
            value = jnp.full(label.shape, table_ref[prop, 0])
            for phase in range(1, table_ref.shape[1]):
                value = jnp.where(label == phase, table_ref[prop, phase], value)
            value = step_dt * value if prop < 2 else step_dt / value
            out[prop] = jnp.where(inside, value, 0.0)

    shape = (LAYERS, wide, LANES)
    r = row_of(shape)
    inside = (r < ROWS) | ((r < ROWS + REACH) & (gx < nx - 1)) | ((r >= ROWS + REACH) & (gx > 0))
    both = jnp.concatenate([lab[0, :, BASE:END, :], halo_rows(lab, 0)], axis=1)
    materials(both, inside, mats)
    lane = lane_of((ROWS, LANES))
    column = lane % 16 + jnp.where(lane % 32 < 16, -8, LANES - 8)
    inside = ((column >= 0) | (gy > 0)) & ((column < LANES) | (gy < ny - 1))
    materials(strip_of(lab_edge[0], lab_side[0, 0], lab_side[1, 0]), inside, mats_s)

    own_mats = lambda prop: mats[prop, :, :ROWS]
    halo_mats = lambda prop: mats[prop, :, ROWS:]
    sxx, sxy, sxz, syy, syz, szz, vx, vy, vz = range(9)
    f_terms = (
        ((sxx, True), (sxy, False), (sxz, False)),
        ((sxy, False), (syy, True), (syz, False)),
        ((sxz, False), (syz, False), (szz, True)),
    )

    def forward_ahead(t):
        slot = t % 2
        for i, (_, (y, y_plus), (z, z_plus)) in enumerate(f_terms):
            terms = ring_diff_y(fwd.own(slot, y), y_plus) + diff_z(fwd.own(slot, z), z_plus)
            part = fwd.own(slot, vx + i) + own_mats(2) * terms
            f_part[i] = part + inj_f[t, :, :ROWS] if i == 2 else part

    def forward_step(t):
        slot, other = t % 2, 1 - t % 2
        buf = f_buf.at[slot]
        fwd.wait_recv(slot)
        tiles = fwd.corner_tiles(slot)
        if t > 0:
            fwd.wait_send(other)
        strips = {}

        def strip(place):
            if place not in strips:
                strips[place] = fwd.strip(slot, place)
            return strips[place]

        for place in (sxx, sxy, sxz):
            fwd.set_strip_rows(place, strip(place), tiles)
        v, ends = [], []
        for i, ((x, x_plus), (y, y_plus), (z, z_plus)) in enumerate(f_terms):
            terms = diff_x(buf, x, x_plus) + fwd.ring_correction(slot, y, y_plus)
            v.append(f_part[i] + own_mats(2) * terms)
            fwd.put(other, vx + i, v[i])
            f_work[i, :, BASE:END, :] = v[i]
            terms = (
                halo_diff_x(buf, x, x_plus)
                + diff_y(halo_rows(buf, y), fwd.corner_y_halo(y, tiles), y_plus)
                + diff_z(halo_rows(buf, z), z_plus)
            )
            new = halo_rows(buf, vx + i) + halo_mats(2) * terms
            put_halo_rows(f_work, i, new + inj_f[t, :, ROWS:] if i == 2 else new)
            terms = (
                strip_x(f_strips, x, x_plus)
                + strip_y(strip(y), y_plus)
                + strip_z(strip(z), z_plus)
            )
            side = strip(vx + i) + mats_s[2] * terms
            ends.append(y_ends_of_strip(side + inj_s[t] if i == 2 else side, i != 1))
        vx_y, vz_y = inner_diff_y((v[0], v[2]), matrices[0])
        (vy_y,) = inner_diff_y((v[1],), matrices[1])
        strain = (
            diff_x(f_work, 0, False),
            vy_y + ends[1],
            diff_z(v[2], False),
            vx_y + ends[0] + diff_x(f_work, 1, True),
            diff_z(v[0], True) + diff_x(f_work, 2, True),
            diff_z(v[1], True) + vz_y + ends[2],
        )
        for i in range(6):
            e_all[t, i] = strain[i]
        if t < steps - 1:
            lam, shear = own_mats(0), own_mats(1)
            exx, eyy, ezz, exy, exz, eyz = strain
            base, twice = lam * (exx + eyy + ezz), 2.0 * shear
            for place, inc in (
                (sxx, base + twice * exx), (sxy, shear * exy), (sxz, shear * exz),
                (syy, base + twice * eyy), (syz, shear * eyz), (szz, base + twice * ezz),
            ):
                fwd.put(other, place, fwd.own(slot, place) + inc)
            fwd.send(other)

    ux, uy, uz, qxx, qxy, qxz, qyy, qyz, qzz = range(9)

    def adjoint_ahead(t):
        u = [adj.own(t % 2, i) for i in range(3)]
        a_part[0] = ring_diff_y(u[1], False)
        a_part[1] = diff_z(u[2], False)
        a_part[2] = ring_diff_y(u[0], True)
        a_part[3] = diff_z(u[0], True)
        a_part[4] = diff_z(u[1], True) + ring_diff_y(u[2], True)

    def adjoint_step(t):
        slot, other = t % 2, 1 - t % 2
        buf = a_buf.at[slot]
        adj.wait_recv(slot)
        tiles = adj.corner_tiles(slot)
        if t > 0:
            adj.wait_send(other)

        def put(place, value):
            if t < steps - 1:
                adj.put(other, place, value)
            else:
                out_ref[ADJ[place]] = value

        side = [adj.strip(slot, i) for i in range(3)]
        for i in range(2):
            adj.set_strip_rows(i, side[i], tiles)
        xx, yy, zz = strip_x(a_strips, ux, False), strip_y(side[1], False), strip_z(side[2], False)
        xy = strip_y(side[0], True) + strip_x(a_strips, uy, True)
        yz = strip_z(side[1], True) + strip_y(side[2], True)
        lam, shear = mats_s[0], mats_s[1]
        ends = {}
        for place, inc in (
            (qxy, shear * xy), (qyy, lam * (xx + yy + zz) + 2.0 * shear * yy), (qyz, shear * yz)
        ):
            ends[place] = y_ends_of_strip(adj.strip(slot, place) - inc, place == qyy)
        u = [halo_rows(buf, i) for i in range(3)]
        u_halo = [adj.corner_y_halo(i, tiles) for i in range(2)]
        exx, eyy = halo_diff_x(buf, ux, False), diff_y(u[1], u_halo[1], False)
        exy = diff_y(u[0], u_halo[0], True) + halo_diff_x(buf, uy, True)
        exz = diff_z(u[0], True) + halo_diff_x(buf, uz, True)
        lam, shear = halo_mats(0), halo_mats(1)
        base = lam * (exx + eyy + diff_z(u[2], False))
        for i, (place, inc) in enumerate(
            ((qxx, base + 2.0 * shear * exx), (qxy, shear * exy), (qxz, shear * exz))
        ):
            put_halo_rows(a_work, i, halo_rows(buf, place) - inc)
        exx, ezz = diff_x(buf, ux, False), a_part[1]
        eyy = a_part[0] + adj.ring_correction(slot, uy, False)
        exy = a_part[2] + adj.ring_correction(slot, ux, True) + diff_x(buf, uy, True)
        exz = a_part[3] + diff_x(buf, uz, True)
        eyz = a_part[4] + adj.ring_correction(slot, uz, True)
        for i, value in enumerate((exx, eyy, ezz, exy, exz, eyz)):
            f_all[t, i] = value
        lam, shear = own_mats(0), own_mats(1)
        base, twice = lam * (exx + eyy + ezz), 2.0 * shear
        q = {}
        for place, inc in (
            (qxx, base + twice * exx), (qxy, shear * exy), (qxz, shear * exz),
            (qyy, base + twice * eyy), (qyz, shear * eyz), (qzz, base + twice * ezz),
        ):
            q[place] = adj.own(slot, place) - inc
            put(place, q[place])
        for i, place in enumerate((qxx, qxy, qxz)):
            a_work[i, :, BASE:END, :] = q[place]
        (qyy_y,) = inner_diff_y((q[qyy],), matrices[0])
        qxy_y, qyz_y = inner_diff_y((q[qxy], q[qyz]), matrices[1])
        div = (
            diff_x(a_work, 0, True) + qxy_y + ends[qxy] + diff_z(q[qxz], False),
            diff_x(a_work, 1, False) + qyy_y + ends[qyy] + diff_z(q[qyz], False),
            diff_x(a_work, 2, False) + qyz_y + ends[qyz] + diff_z(q[qzz], True),
        )
        for i in range(3):
            value = adj.own(slot, i) - own_mats(2) * div[i]
            put(i, value + inj_a[t] if i == 2 else value)
        if t < steps - 1:
            adj.send(other)

    for t in range(steps):
        forward_ahead(t)
        adjoint_ahead(t)
        forward_step(t)
        adjoint_step(t)

    last = (steps - 1) % 2
    fwd.wait_send(last)
    adj.wait_send(last)
    for goes, _, copy in lab_copies:
        pl.when(goes)(copy.wait_send)

    grad_l = grad_m = None
    for t in range(steps):
        e = [e_all[steps - 1 - t, i] for i in range(6)]
        f = [f_all[t, i] for i in range(6)]
        more_l = (e[0] + e[1] + e[2]) * (f[0] + f[1] + f[2])
        more_m = 2.0 * (e[0] * f[0] + e[1] * f[1] + e[2] * f[2])
        more_m = more_m + e[3] * f[3] + e[4] * f[4] + e[5] * f[5]
        grad_l = more_l if grad_l is None else grad_l + more_l
        grad_m = more_m if grad_m is None else grad_m + more_m
    gl_ref[...] = step_dt * grad_l
    gm_ref[...] = step_dt * grad_m


def hand_over(*refs):
    sem = refs[-1]
    copies = [pltpu.make_async_copy(refs[i], refs[3 + i], sem.at[i]) for i in range(3)]
    for copy in copies:
        copy.start()
    for copy in copies:
        copy.wait()


def shards(fwd, adj, labels, table, src, wav, rec, res):
    assert labels.shape == (LAYERS, ROWS, LANES)
    dims = (ROWS * lax.axis_size("gx"), LANES * lax.axis_size("gy"))
    steps = wav.shape[0]
    f32 = jnp.float32
    block, tile = (LAYERS, ROWS, LANES), (SUB, LANES)
    wide = (LAYERS, ROWS + SUB, LANES)

    def vmem(*shape):
        return pltpu.VMEM(shape, f32)

    def chain(edges, corners, strips):
        return [
            vmem(2, 9, LAYERS, PADDED, LANES),
            vmem(2, edges, *tile),
            vmem(2, 2, edges, *tile),
            vmem(2, corners, *tile),
            vmem(2, 4, corners, *tile),
            vmem(strips, PADDED, LANES),
        ]

    in_hbm = pl.BlockSpec(memory_space=pl.ANY)
    in_vmem = pl.BlockSpec(memory_space=pltpu.VMEM)
    dma = pltpu.SemaphoreType.DMA
    operands = [
        pltpu.with_memory_space_constraint(x, pltpu.HBM)
        for x in (fwd, adj, labels, table, src.reshape(1, -1), wav, rec.reshape(1, -1), res)
    ]
    results = pl.pallas_call(
        functools.partial(kernel, dims),
        out_shape=(
            pltpu.VMEM(fwd.shape, f32),
            pltpu.VMEM(block, f32),
            pltpu.VMEM(block, f32),
        ),
        in_specs=[in_hbm] * 8,
        out_specs=(in_vmem, in_vmem, in_vmem),
        scratch_shapes=[
            pltpu.SMEM(table.shape, f32),
            pltpu.VMEM((1,) + src.shape, jnp.int32),
            vmem(*wav.shape),
            pltpu.VMEM((1,) + rec.shape, jnp.int32),
            vmem(*res.shape),
        ] + chain(9, 2, 3) + chain(6, 1, 2) + [
            vmem(2, LANES, LANES),
            vmem(3, LAYERS, PADDED, LANES),
            vmem(3, LAYERS, PADDED, LANES),
            vmem(3, *block),
            vmem(5, *block),
            pltpu.VMEM(block, jnp.int32),
            vmem(1, LAYERS, PADDED, LANES),
            vmem(1, *tile),
            vmem(2, 1, *tile),
            vmem(3, *wide),
            vmem(3, ROWS, LANES),
            vmem(steps, *wide),
            vmem(steps, ROWS, LANES),
            vmem(steps, *block),
            vmem(steps, 6, *block),
            vmem(steps, 6, *block),
            vmem(2, *block),
            dma((24,)), dma((11,)),
            dma((2, 10)), dma((2, 10)), dma((2, 10)), dma((2, 10)),
            dma((4,)), dma((4,)),
        ],
        compiler_params=pltpu.CompilerParams(
            collective_id=0, has_side_effects=True, vmem_limit_bytes=40 * 1024 * 1024
        ),
    )(*operands)
    return pl.pallas_call(
        hand_over,
        out_shape=(
            pltpu.HBM(fwd.shape, f32),
            pltpu.HBM(block, f32),
            pltpu.HBM(block, f32),
        ),
        in_specs=[in_hbm] * 3,
        out_specs=(in_hbm,) * 3,
        scratch_shapes=[dma((3,))],
    )(*(pltpu.with_memory_space_constraint(r, pltpu.VMEM) for r in results))


def solution(mesh):
    state, cells = P(None, None, "gx", "gy"), P(None, "gx", "gy")
    return jax.shard_map(
        shards,
        mesh=mesh,
        in_specs=(state, state, cells, P(), P(), P(), P(), P()),
        out_specs=(state, cells, cells),
        check_vma=False,
    )
```

```python
import functools

import jax
import jax.numpy as jnp
from jax import lax
from jax.experimental import pallas as pl
from jax.experimental.pallas import tpu as pltpu
from jax.sharding import PartitionSpec as P

coeffs = (1225.0 / 1024.0, -245.0 / 3072.0, 49.0 / 5120.0, -5.0 / 7168.0)
step_dt = 0.1
MESH = pl.DeviceIdType.MESH

LAYERS, ROWS, LANES, SUB = 4, 16, 128, 8
REACH = 4
BASE = 16
PADDED = ROWS + 2 * BASE
END = BASE + ROWS

FWD = (3, 6, 7, 4, 8, 5, 0, 1, 2)
ADJ = (0, 1, 2, 3, 6, 7, 4, 8, 5)
FWD_EDGES = tuple(range(9))
ADJ_EDGES = (0, 1, 2, 4, 6, 7)
FWD_CORNERS = (1, 3, 4, 0, 2)
ADJ_CORNERS = (0, 1)


def place_in_grid():
    gx, gy = lax.axis_index("gx"), lax.axis_index("gy")
    return gx, gy, lax.axis_size("gx"), lax.axis_size("gy")


def neighbours():
    gx, gy, nx, ny = place_in_grid()
    xs = {-1: lax.rem(gx + nx - 1, nx), 0: gx, 1: lax.rem(gx + 1, nx)}
    ys = {-1: lax.rem(gy + ny - 1, ny), 0: gy, 1: lax.rem(gy + 1, ny)}
    in_x, in_y = {-1: gx > 0, 1: gx < nx - 1}, {-1: gy > 0, 1: gy < ny - 1}
    out = {}
    for dx in (-1, 0, 1):
        for dy in (-1, 0, 1):
            if dx and dy:
                out[dx, dy] = (xs[dx], ys[dy]), jnp.logical_and(in_x[dx], in_y[dy])
            elif dx or dy:
                out[dx, dy] = (xs[dx], ys[dy]), in_x[dx] if dx else in_y[dy]
    return out


def lane_of(shape):
    return lax.broadcasted_iota(jnp.int32, shape, len(shape) - 1)


def row_of(shape):
    return lax.broadcasted_iota(jnp.int32, shape, len(shape) - 2)


def roll(value, by):
    by %= LANES
    return value if by == 0 else pltpu.roll(value, by, value.ndim - 1)


def weighted(shift, plus):
    total = None
    for k in range(1, REACH + 1):
        first = k if plus else k - 1
        term = coeffs[k - 1] * (shift(first) - shift(first + 1 - 2 * k))
        total = term if total is None else total + term
    return total


def halo_rows(buf, field, d=0):
    after = buf[field, :, END + d : END + d + SUB, :]
    before = buf[field, :, BASE - SUB + d : BASE + d, :]
    return jnp.where(row_of(after.shape) < REACH, after, before)


def halo_diff_x(buf, field, plus):
    return weighted(lambda d: halo_rows(buf, field, d), plus)


def diff_x(buf, field, plus):
    return weighted(lambda d: buf[field, :, BASE + d : END + d, :], plus)


def near_and_far(shift, plus):
    sign = -1 if plus else 1
    taps = [shift(sign * k) for k in range(REACH)]
    near = far = None
    for k in range(REACH):
        one, two = coeffs[k] * taps[k], coeffs[REACH - 1 - k] * taps[k]
        near = one if near is None else near + one
        far = two if far is None else far + two
    return near, far


def ring_diff_y(field, plus):
    near, far = near_and_far(lambda d: roll(field, -d), plus)
    return roll(far, -REACH) - near if plus else near - roll(far, REACH)


def diff_z(field, plus):
    out = []
    for i in range(LAYERS):
        total = None
        for k in range(1, REACH + 1):
            first = i + (k if plus else k - 1)
            second = first + 1 - 2 * k
            has_first, has_second = 0 <= first < LAYERS, 0 <= second < LAYERS
            if has_first and has_second:
                term = coeffs[k - 1] * (field[first] - field[second])
            elif has_first:
                term = coeffs[k - 1] * field[first]
            elif has_second:
                term = -coeffs[k - 1] * field[second]
            else:
                continue
            total = term if total is None else total + term
        out.append(total)
    return jnp.stack(out)


def strip_x(buf, field, plus):
    return weighted(lambda d: buf[field, BASE + d : END + d, :], plus)


strip_y = ring_diff_y


def strip_z(field, plus):
    layer = lane_of(field.shape) // 32
    weights = {}
    for k in range(1, REACH + 1):
        first = k if plus else k - 1
        weights[first] = weights.get(first, 0.0) + coeffs[k - 1]
        weights[first + 1 - 2 * k] = weights.get(first + 1 - 2 * k, 0.0) - coeffs[k - 1]
    total = None
    for d, weight in weights.items():
        if abs(d) >= LAYERS:
            continue
        inside = (layer + d >= 0) & (layer + d < LAYERS)
        term = jnp.where(inside, weight, 0.0) * roll(field, -32 * d)
        total = term if total is None else total + term
    return total


def pack_edge(field):
    group = lane_of((SUB, LANES)) // 16
    packed = None
    for z in range(LAYERS):
        for tile in range(2):
            at = 2 * z + tile
            piece = roll(field[z, SUB * tile : SUB * (tile + 1)], 8 + 16 * at)
            packed = piece if packed is None else jnp.where(group == at, piece, packed)
    return packed


def pack_corners(edges, out_ref, slot):
    group = lane_of((SUB, LANES)) // 8 % 4
    top = row_of((SUB, LANES)) < REACH
    for start in range(0, len(edges), 4):
        packed = None
        for g, edge in enumerate(edges[start : start + 4]):
            piece = jnp.where(top, roll(edge, 8 * g - 4), roll(edge, 8 * g - 20))
            packed = piece if packed is None else jnp.where(group == g, piece, packed)
        out_ref[slot, start // 4] = packed


def strip_of(edge, low, high):
    half = lane_of(edge.shape) % 16 < 8
    first, last = jnp.where(half, low, edge), jnp.where(half, edge, high)
    side = lane_of(edge.shape) % 32 < 16
    tiles = [jnp.where(side, first, roll(last, 16)), jnp.where(side, roll(first, -16), last)]
    return jnp.concatenate(tiles, axis=0)


def end_terms(lack, plus):
    p = lane_of(lack.shape) % 16
    before, after = jnp.where(p < 8, lack, 0.0), jnp.where(p < 8, 0.0, lack)
    first_lanes = last_lanes = None
    for k in range(1, REACH + 1):
        first = k if plus else k - 1
        second = first + 1 - 2 * k
        if first > 0:
            term = coeffs[k - 1] * roll(after, -first)
            last_lanes = term if last_lanes is None else last_lanes + term
        if second < 0:
            term = coeffs[k - 1] * roll(before, -second)
            first_lanes = -term if first_lanes is None else first_lanes - term
    return jnp.where(p < 8, last_lanes, first_lanes)


def at_ends(value):
    lane = lane_of(value.shape)
    return jnp.where((lane < REACH) | (lane >= LANES - REACH), value, 0.0)


def ring_correction(edge, low, high, plus):
    total = end_terms(jnp.where(lane_of(edge.shape) % 16 < 8, low, high) - edge, plus)
    return jnp.stack([
        jnp.concatenate([at_ends(roll(total, 120 - 32 * z - 16 * t)) for t in range(2)], axis=0)
        for z in range(LAYERS)
    ])


def y_ends_of_strip(strip, plus):
    merged = jnp.where(lane_of(strip.shape) % 16 < 8, strip, roll(strip, -16))
    total = end_terms(merged, plus)
    return jnp.stack([at_ends(roll(total, 120 - 32 * z)) for z in range(LAYERS)])


def stencil_matrix(plus):
    source = lax.broadcasted_iota(jnp.int32, (LANES, LANES), 0)
    off = source - lane_of((LANES, LANES))
    total = jnp.zeros((LANES, LANES), jnp.float32)
    for k in range(1, REACH + 1):
        first = k if plus else k - 1
        total = jnp.where(off == first, coeffs[k - 1], total)
        total = jnp.where(off == first + 1 - 2 * k, -coeffs[k - 1], total)
    return total


def inner_diff_y(fields, matrix):
    shape = fields[0].shape
    rows = shape[0] * shape[1]
    stacked = jnp.concatenate([f.reshape(rows, LANES) for f in fields], axis=0)
    out = jnp.dot(
        stacked, matrix, precision=lax.Precision.HIGHEST, preferred_element_type=jnp.float32
    )
    return [out[i * rows : (i + 1) * rows].reshape(shape) for i in range(len(fields))]


def corner_end_terms(corner):
    first = lane_of(corner.shape) % 8 < 4
    before, after = jnp.where(first, corner, 0.0), jnp.where(first, 0.0, corner)
    back = [None] + [roll(before, k) for k in range(1, REACH + 1)]
    ahead = [None] + [roll(after, -k) for k in range(1, REACH + 1)]

    def total(terms, shift):
        pairs = [(c, terms[k]) for k, c in enumerate(coeffs, shift) if k > 0]
        return sum((c * term for c, term in pairs[1:]), pairs[0][0] * pairs[0][1])

    p_stencil = jnp.where(first, total(ahead, 1), -total(back, 0))
    m_stencil = jnp.where(first, total(ahead, 0), -total(back, 1))
    return p_stencil, m_stencil


def strip_rows_of_corners(corner, g):
    side = lane_of(corner.shape) % 32 < 16
    return jnp.where(side, roll(corner, 4 - 8 * g), roll(corner, 20 - 8 * g))


class Chain:
    def __init__(self, refs, around, deep, shallow, edges, corners):
        self.around = around
        (self.buf, self.edge, self.side, self.corner, self.corners_in,
         self.strips, self.send_sem, self.recv_sem) = refs
        self.deep, self.shallow = deep, shallow
        self.edges, self.corner_places = edges, corners

    def copies(self, slot):
        out = []

        def add(dx, dy, src, dst):
            to, goes = self.around[dx, dy]
            _, arrives = self.around[-dx, -dy]
            copy = pltpu.make_async_remote_copy(
                src_ref=src,
                dst_ref=dst,
                send_sem=self.send_sem.at[slot, len(out)],
                recv_sem=self.recv_sem.at[slot, len(out)],
                device_id=to,
                device_id_type=MESH,
            )
            out.append((goes, arrives, copy))

        for dx in (-1, 1):
            for dy in (-1, 1):
                at = (1 - dx) // 2 * 2 + (1 - dy) // 2
                add(dx, dy, self.corner.at[slot], self.corners_in.at[slot, at])
        for dy in (-1, 1):
            add(0, dy, self.edge.at[slot], self.side.at[slot, (1 - dy) // 2])
        for fields, count in ((self.deep, SUB), (self.shallow, REACH)):
            for dx in (-1, 1):
                src = BASE if dx < 0 else END - count
                dst = END if dx < 0 else BASE - count
                part = pl.ds(fields[0], len(fields))
                add(dx, 0, self.buf.at[slot, part, :, pl.ds(src, count), :],
                    self.buf.at[slot, part, :, pl.ds(dst, count), :])
        return out

    def clear(self):
        for slot in range(2):
            for fields, count in ((self.deep, SUB), (self.shallow, REACH)):
                zero = jnp.zeros((len(fields), LAYERS, count, LANES), jnp.float32)
                part = pl.ds(fields[0], len(fields))
                self.buf[slot, part, :, BASE - count : BASE, :] = zero
                self.buf[slot, part, :, END : END + count, :] = zero
        self.side[...] = jnp.zeros_like(self.side)
        self.corners_in[...] = jnp.zeros_like(self.corners_in)

    def pack(self, slot):
        edges = []
        for place in self.corner_places:
            edges.append(pack_edge(self.own(slot, place)))
            self.edge[slot, self.edges.index(place)] = edges[-1]
        pack_corners(edges, self.corner, slot)

    def pack_rest(self, slot):
        for i, place in enumerate(self.edges):
            if place not in self.corner_places:
                self.edge[slot, i] = pack_edge(self.own(slot, place))

    def start(self, slot, first, last):
        for goes, _, copy in self.copies(slot)[first:last]:
            pl.when(goes)(copy.start)

    def send(self, slot):
        self.pack(slot)
        self.start(slot, 0, 4)
        self.start(slot, 6, 10)
        self.pack_rest(slot)
        self.start(slot, 4, 6)

    def wait_recv(self, slot):
        for _, arrives, copy in self.copies(slot):
            pl.when(arrives)(copy.wait_recv)

    def wait_send(self, slot):
        for goes, _, copy in self.copies(slot):
            pl.when(goes)(copy.wait_send)

    def own(self, slot, place):
        return self.buf[slot, place, :, BASE:END, :]

    def put(self, slot, place, value):
        self.buf[slot, place, :, BASE:END, :] = value

    def strip(self, slot, place):
        i = self.edges.index(place)
        return strip_of(self.edge[slot, i], self.side[slot, 0, i], self.side[slot, 1, i])

    def ring_correction(self, slot, place, plus):
        i = self.edges.index(place)
        return ring_correction(
            self.edge[slot, i], self.side[slot, 0, i], self.side[slot, 1, i], plus
        )

    def corner_tiles(self, slot):
        shape = (SUB, LANES)
        first, top = lane_of(shape) % 8 < 4, row_of(shape) < REACH
        out = []
        for i in range(self.corner.shape[1]):
            here = [self.corners_in[slot, at, i] for at in range(4)]
            out.append(jnp.where(top, jnp.where(first, here[2], here[3]),
                                 jnp.where(first, here[0], here[1])))
        return out

    def corner_ends(self, place, totals):
        g = self.corner_places.index(place)
        return jnp.stack([at_ends(roll(totals, 124 - 32 * z - 8 * g)) for z in range(LAYERS)])

    def set_strip_rows(self, place, strip, tiles):
        at = self.corner_places.index(place)
        rows = strip_rows_of_corners(tiles[at // 4], at % 4)
        self.strips[place, BASE:END, :] = strip
        self.strips[place, BASE - SUB : BASE, :] = rows
        self.strips[place, END : END + SUB, :] = rows


def put_halo_rows(work, place, value):
    work[place, :, END : END + REACH, :] = value[:, :REACH]
    work[place, :, BASE - REACH : BASE, :] = value[:, REACH:]


def log2(n):
    assert n > 0 and n & (n - 1) == 0
    return n.bit_length() - 1


def spread(traces_ref, row, lane, rows, store):
    steps, count = traces_ref.shape
    row_hit = lax.broadcasted_iota(jnp.int32, (rows, count), 0) == row
    lane_hit = lax.broadcasted_iota(jnp.int32, (LANES, count), 0) == lane
    lanes = jnp.where(lane_hit, 1.0, 0.0).astype(jnp.bfloat16)
    for t in range(steps):
        rest = traces_ref[t : t + 1, :]
        total = None
        for _ in range(3):
            piece = rest.astype(jnp.bfloat16).astype(jnp.float32)
            rest = rest - piece
            left = jnp.where(row_hit, piece, 0.0).astype(jnp.bfloat16)
            part = lax.dot_general(
                left, lanes, (((1,), (1,)), ((), ())), preferred_element_type=jnp.float32
            )
            total = part if total is None else total + part
        store(t, step_dt * total)


def positions(cells_ref, nx_cells, ny_cells):
    gx, gy, _, _ = place_in_grid()
    cells = cells_ref[...]
    layer = lax.shift_right_logical(cells, jnp.int32(log2(nx_cells * ny_cells)))
    at_x = lax.shift_right_logical(cells, jnp.int32(log2(ny_cells))) & (nx_cells - 1)
    return layer, at_x - gx * ROWS, (cells & (ny_cells - 1)) - gy * LANES


def kernel(
    dims,
    fwd_hbm, adj_hbm, labels_hbm, table_hbm, src_hbm, wav_hbm, rec_hbm, res_hbm,
    out_ref, gl_ref, gm_ref,
    table_ref, src_ref, wav_ref, rec_ref, res_ref,
    f_buf, f_edge, f_side, f_corner, f_corners_in, f_strips,
    a_buf, a_edge, a_side, a_corner, a_corners_in, a_strips,
    matrices, f_work, a_work, f_part, a_part, labels, lab, lab_edge, lab_side, mats, mats_s,
    inj_f, inj_s, inj_a, e_all, f_all, grads,
    in_sem, out_sem, f_send, f_recv, a_send, a_recv, l_send, l_recv,
):
    nx_cells, ny_cells = dims
    gx, gy, nx, ny = place_in_grid()
    steps = wav_ref.shape[0]

    around = neighbours()
    fwd = Chain((f_buf, f_edge, f_side, f_corner, f_corners_in, f_strips, f_send, f_recv),
                around, (0, 1, 2), (3, 4, 5, 6, 7, 8), FWD_EDGES, FWD_CORNERS)
    adj = Chain((a_buf, a_edge, a_side, a_corner, a_corners_in, a_strips, a_send, a_recv),
                around, (0, 1, 2), (3, 4, 5), ADJ_EDGES, ADJ_CORNERS)

    fwd.clear()
    adj.clear()
    lab[...] = jnp.zeros_like(lab)
    lab_side[...] = jnp.zeros_like(lab_side)
    barrier = pltpu.get_barrier_semaphore()
    for to, _ in around.values():
        pl.semaphore_signal(barrier, inc=1, device_id=to, device_id_type=MESH)

    loads = []

    def load(src, dst):
        copy = pltpu.make_async_copy(src, dst, in_sem.at[len(loads)])
        copy.start()
        loads.append(copy)

    own_rows = pl.ds(BASE, ROWS)
    load(labels_hbm, labels)
    for hbm, buf, order in ((fwd_hbm, f_buf, FWD), (adj_hbm, a_buf, ADJ)):
        start = 0
        for end in range(1, len(order) + 1):
            if end == len(order) or order[end] != order[end - 1] + 1:
                part = pl.ds(order[start], end - start)
                load(hbm.at[part], buf.at[0, pl.ds(start, end - start), :, own_rows, :])
                start = end
    first = len(loads)
    for src, dst in (
        (table_hbm, table_ref), (src_hbm, src_ref), (wav_hbm, wav_ref),
        (rec_hbm, rec_ref), (res_hbm, res_ref),
    ):
        load(src, dst)

    loads[0].wait()
    lab[0, :, BASE:END, :] = labels[...].astype(jnp.float32)
    lab_edge[0] = pack_edge(lab[0, :, BASE:END, :])
    lab_copies = []
    own_labels = lab.at[0]
    for dx, dy, src, dst in (
        (-1, 0, own_labels.at[:, pl.ds(BASE, REACH), :], own_labels.at[:, pl.ds(END, REACH), :]),
        (1, 0, own_labels.at[:, pl.ds(END - REACH, REACH), :], own_labels.at[:, pl.ds(BASE - REACH, REACH), :]),
        (0, -1, lab_edge, lab_side.at[1]),
        (0, 1, lab_edge, lab_side.at[0]),
    ):
        to, goes = around[dx, dy]
        copy = pltpu.make_async_remote_copy(
            src_ref=src, dst_ref=dst, send_sem=l_send.at[len(lab_copies)],
            recv_sem=l_recv.at[len(lab_copies)], device_id=to, device_id_type=MESH,
        )
        lab_copies.append((goes, around[-dx, -dy][1], copy))

    for copy in loads[1:first]:
        copy.wait()
    for chain in (fwd, adj):
        chain.pack(0)
        chain.pack_rest(0)
    pl.semaphore_wait(barrier, len(around))
    fwd.start(0, 0, 10)
    adj.start(0, 0, 10)
    for goes, _, copy in lab_copies:
        pl.when(goes)(copy.start)

    for copy in loads[first:]:
        copy.wait()
    layer, at_x, at_y = positions(src_ref, nx_cells, ny_cells)
    wide = ROWS + SUB
    here = jnp.where(at_x < 0, at_x + wide, at_x)
    row = jnp.where((at_x >= -REACH) & (at_x < ROWS + REACH), layer * wide + here, -1)

    def store_wide(t, value):
        inj_f[t] = value.reshape(LAYERS, wide, LANES)

    spread(wav_ref, row, at_y, LAYERS * wide, store_wide)
    column = jnp.where((at_y >= -REACH) & (at_y < 0), 32 * layer + 8 + at_y, -1)
    column = jnp.where((at_y >= LANES) & (at_y < LANES + REACH), 32 * layer + 24 + at_y - LANES, column)

    def store_strip(t, value):
        inj_s[t] = value

    spread(wav_ref, at_x, column, ROWS, store_strip)
    layer, at_x, at_y = positions(rec_ref, nx_cells, ny_cells)
    row = jnp.where((at_x >= 0) & (at_x < ROWS), layer * ROWS + at_x, -1)

    def store_own(t, value):
        inj_a[t] = value.reshape(LAYERS, ROWS, LANES)

    spread(res_ref, row, at_y, LAYERS * ROWS, store_own)

    matrices[0] = stencil_matrix(True)
    matrices[1] = stencil_matrix(False)

    for _, arrives, copy in lab_copies:
        pl.when(arrives)(copy.wait_recv)

    def materials(label, inside, out):
        for prop in range(3):
            value = jnp.full(label.shape, table_ref[prop, 0])
            for phase in range(1, table_ref.shape[1]):
                value = jnp.where(label == phase, table_ref[prop, phase], value)
            value = step_dt * value if prop < 2 else step_dt / value
            out[prop] = jnp.where(inside, value, 0.0)

    shape = (LAYERS, wide, LANES)
    r = row_of(shape)
    inside = (r < ROWS) | ((r < ROWS + REACH) & (gx < nx - 1)) | ((r >= ROWS + REACH) & (gx > 0))
    both = jnp.concatenate([lab[0, :, BASE:END, :], halo_rows(lab, 0)], axis=1)
    materials(both, inside, mats)
    lane = lane_of((ROWS, LANES))
    column = lane % 16 + jnp.where(lane % 32 < 16, -8, LANES - 8)
    inside = ((column >= 0) | (gy > 0)) & ((column < LANES) | (gy < ny - 1))
    materials(strip_of(lab_edge[0], lab_side[0, 0], lab_side[1, 0]), inside, mats_s)

    own_mats = lambda prop: mats[prop, :, :ROWS]
    halo_mats = lambda prop: mats[prop, :, ROWS:]
    sxx, sxy, sxz, syy, syz, szz, vx, vy, vz = range(9)
    f_terms = (
        ((sxx, True), (sxy, False), (sxz, False)),
        ((sxy, False), (syy, True), (syz, False)),
        ((sxz, False), (syz, False), (szz, True)),
    )

    def forward_ahead(t):
        slot = t % 2
        if t > 0:
            fwd.wait_send(1 - slot)
        for i, (_, (y, y_plus), (z, z_plus)) in enumerate(f_terms):
            terms = ring_diff_y(fwd.own(slot, y), y_plus) + diff_z(fwd.own(slot, z), z_plus)
            part = fwd.own(slot, vx + i) + own_mats(2) * terms
            f_part[i] = part + inj_f[t, :, :ROWS] if i == 2 else part

    def forward_step(t):
        slot, other = t % 2, 1 - t % 2
        buf = f_buf.at[slot]
        fwd.wait_recv(slot)
        tiles = fwd.corner_tiles(slot)
        strips = {}

        def strip(place):
            if place not in strips:
                strips[place] = fwd.strip(slot, place)
            return strips[place]

        for place in (sxx, sxy, sxz):
            fwd.set_strip_rows(place, strip(place), tiles)
        p_ends, m_ends = corner_end_terms(tiles[0])
        halo_y = dict(zip((syy,), inner_diff_y((halo_rows(buf, syy),), matrices[0])))
        halo_y.update(zip((sxy, syz), inner_diff_y(
            (halo_rows(buf, sxy), halo_rows(buf, syz)), matrices[1])))
        v, ends = [], []
        for i, ((x, x_plus), (y, y_plus), (z, z_plus)) in enumerate(f_terms):
            terms = diff_x(buf, x, x_plus) + fwd.ring_correction(slot, y, y_plus)
            v.append(f_part[i] + own_mats(2) * terms)
            fwd.put(other, vx + i, v[i])
            f_work[i, :, BASE:END, :] = v[i]
            terms = (
                halo_diff_x(buf, x, x_plus)
                + halo_y[y] + fwd.corner_ends(y, p_ends if y_plus else m_ends)
                + diff_z(halo_rows(buf, z), z_plus)
            )
            new = halo_rows(buf, vx + i) + halo_mats(2) * terms
            put_halo_rows(f_work, i, new + inj_f[t, :, ROWS:] if i == 2 else new)
            terms = (
                strip_x(f_strips, x, x_plus)
                + strip_y(strip(y), y_plus)
                + strip_z(strip(z), z_plus)
            )
            side = strip(vx + i) + mats_s[2] * terms
            ends.append(y_ends_of_strip(side + inj_s[t] if i == 2 else side, i != 1))
        vx_y, vz_y = inner_diff_y((v[0], v[2]), matrices[0])
        (vy_y,) = inner_diff_y((v[1],), matrices[1])
        strain = (
            diff_x(f_work, 0, False),
            vy_y + ends[1],
            diff_z(v[2], False),
            vx_y + ends[0] + diff_x(f_work, 1, True),
            diff_z(v[0], True) + diff_x(f_work, 2, True),
            diff_z(v[1], True) + vz_y + ends[2],
        )
        for i in range(6):
            e_all[t, i] = strain[i]
        if t < steps - 1:
            lam, shear = own_mats(0), own_mats(1)
            exx, eyy, ezz, exy, exz, eyz = strain
            base, twice = lam * (exx + eyy + ezz), 2.0 * shear
            for place, inc in (
                (sxx, base + twice * exx), (sxy, shear * exy), (sxz, shear * exz),
                (syy, base + twice * eyy), (syz, shear * eyz), (szz, base + twice * ezz),
            ):
                fwd.put(other, place, fwd.own(slot, place) + inc)
            fwd.send(other)

    ux, uy, uz, qxx, qxy, qxz, qyy, qyz, qzz = range(9)

    def adjoint_ahead(t):
        if t > 0:
            adj.wait_send(1 - t % 2)
        u = [adj.own(t % 2, i) for i in range(3)]
        a_part[0] = ring_diff_y(u[1], False)
        a_part[1] = diff_z(u[2], False)
        a_part[2] = ring_diff_y(u[0], True)
        a_part[3] = diff_z(u[0], True)
        a_part[4] = diff_z(u[1], True) + ring_diff_y(u[2], True)

    def adjoint_step(t):
        slot, other = t % 2, 1 - t % 2
        buf = a_buf.at[slot]
        adj.wait_recv(slot)
        tiles = adj.corner_tiles(slot)

        def put(place, value):
            if t < steps - 1:
                adj.put(other, place, value)
            else:
                out_ref[ADJ[place]] = value

        side = [adj.strip(slot, i) for i in range(3)]
        for i in range(2):
            adj.set_strip_rows(i, side[i], tiles)
        xx, yy, zz = strip_x(a_strips, ux, False), strip_y(side[1], False), strip_z(side[2], False)
        xy = strip_y(side[0], True) + strip_x(a_strips, uy, True)
        yz = strip_z(side[1], True) + strip_y(side[2], True)
        lam, shear = mats_s[0], mats_s[1]
        ends = {}
        for place, inc in (
            (qxy, shear * xy), (qyy, lam * (xx + yy + zz) + 2.0 * shear * yy), (qyz, shear * yz)
        ):
            ends[place] = y_ends_of_strip(adj.strip(slot, place) - inc, place == qyy)
        u = [halo_rows(buf, i) for i in range(3)]
        p_ends, m_ends = corner_end_terms(tiles[0])
        (ux_y,), (uy_y,) = inner_diff_y((u[0],), matrices[0]), inner_diff_y((u[1],), matrices[1])
        exx, eyy = halo_diff_x(buf, ux, False), uy_y + adj.corner_ends(uy, m_ends)
        exy = ux_y + adj.corner_ends(ux, p_ends) + halo_diff_x(buf, uy, True)
        exz = diff_z(u[0], True) + halo_diff_x(buf, uz, True)
        lam, shear = halo_mats(0), halo_mats(1)
        base = lam * (exx + eyy + diff_z(u[2], False))
        for i, (place, inc) in enumerate(
            ((qxx, base + 2.0 * shear * exx), (qxy, shear * exy), (qxz, shear * exz))
        ):
            put_halo_rows(a_work, i, halo_rows(buf, place) - inc)
        exx, ezz = diff_x(buf, ux, False), a_part[1]
        eyy = a_part[0] + adj.ring_correction(slot, uy, False)
        exy = a_part[2] + adj.ring_correction(slot, ux, True) + diff_x(buf, uy, True)
        exz = a_part[3] + diff_x(buf, uz, True)
        eyz = a_part[4] + adj.ring_correction(slot, uz, True)
        for i, value in enumerate((exx, eyy, ezz, exy, exz, eyz)):
            f_all[t, i] = value
        lam, shear = own_mats(0), own_mats(1)
        base, twice = lam * (exx + eyy + ezz), 2.0 * shear
        q = {}
        for place, inc in (
            (qxx, base + twice * exx), (qxy, shear * exy), (qxz, shear * exz),
            (qyy, base + twice * eyy), (qyz, shear * eyz), (qzz, base + twice * ezz),
        ):
            q[place] = adj.own(slot, place) - inc
            put(place, q[place])
        for i, place in enumerate((qxx, qxy, qxz)):
            a_work[i, :, BASE:END, :] = q[place]
        (qyy_y,) = inner_diff_y((q[qyy],), matrices[0])
        qxy_y, qyz_y = inner_diff_y((q[qxy], q[qyz]), matrices[1])
        div = (
            diff_x(a_work, 0, True) + qxy_y + ends[qxy] + diff_z(q[qxz], False),
            diff_x(a_work, 1, False) + qyy_y + ends[qyy] + diff_z(q[qyz], False),
            diff_x(a_work, 2, False) + qyz_y + ends[qyz] + diff_z(q[qzz], True),
        )
        for i in range(3):
            value = adj.own(slot, i) - own_mats(2) * div[i]
            put(i, value + inj_a[t] if i == 2 else value)
        if t < steps - 1:
            adj.send(other)

    for t in range(steps):
        forward_ahead(t)
        adjoint_ahead(t)
        forward_step(t)
        adjoint_step(t)

    last = (steps - 1) % 2
    fwd.wait_send(last)
    adj.wait_send(last)
    for goes, _, copy in lab_copies:
        pl.when(goes)(copy.wait_send)

    grad_l = grad_m = None
    for t in range(steps):
        e = [e_all[steps - 1 - t, i] for i in range(6)]
        f = [f_all[t, i] for i in range(6)]
        more_l = (e[0] + e[1] + e[2]) * (f[0] + f[1] + f[2])
        more_m = 2.0 * (e[0] * f[0] + e[1] * f[1] + e[2] * f[2])
        more_m = more_m + e[3] * f[3] + e[4] * f[4] + e[5] * f[5]
        grad_l = more_l if grad_l is None else grad_l + more_l
        grad_m = more_m if grad_m is None else grad_m + more_m
    gl_ref[...] = step_dt * grad_l
    gm_ref[...] = step_dt * grad_m


def hand_over(*refs):
    sem = refs[-1]
    copies = [pltpu.make_async_copy(refs[i], refs[3 + i], sem.at[i]) for i in range(3)]
    for copy in copies:
        copy.start()
    for copy in copies:
        copy.wait()


def shards(fwd, adj, labels, table, src, wav, rec, res):
    assert labels.shape == (LAYERS, ROWS, LANES)
    dims = (ROWS * lax.axis_size("gx"), LANES * lax.axis_size("gy"))
    steps = wav.shape[0]
    f32 = jnp.float32
    block, tile = (LAYERS, ROWS, LANES), (SUB, LANES)
    wide = (LAYERS, ROWS + SUB, LANES)

    def vmem(*shape):
        return pltpu.VMEM(shape, f32)

    def chain(edges, corners, strips):
        return [
            vmem(2, 9, LAYERS, PADDED, LANES),
            vmem(2, edges, *tile),
            vmem(2, 2, edges, *tile),
            vmem(2, corners, *tile),
            vmem(2, 4, corners, *tile),
            vmem(strips, PADDED, LANES),
        ]

    in_hbm = pl.BlockSpec(memory_space=pl.ANY)
    in_vmem = pl.BlockSpec(memory_space=pltpu.VMEM)
    dma = pltpu.SemaphoreType.DMA
    operands = [
        pltpu.with_memory_space_constraint(x, pltpu.HBM)
        for x in (fwd, adj, labels, table, src.reshape(1, -1), wav, rec.reshape(1, -1), res)
    ]
    results = pl.pallas_call(
        functools.partial(kernel, dims),
        out_shape=(
            pltpu.VMEM(fwd.shape, f32),
            pltpu.VMEM(block, f32),
            pltpu.VMEM(block, f32),
        ),
        in_specs=[in_hbm] * 8,
        out_specs=(in_vmem, in_vmem, in_vmem),
        scratch_shapes=[
            pltpu.SMEM(table.shape, f32),
            pltpu.VMEM((1,) + src.shape, jnp.int32),
            vmem(*wav.shape),
            pltpu.VMEM((1,) + rec.shape, jnp.int32),
            vmem(*res.shape),
        ] + chain(9, 2, 3) + chain(6, 1, 2) + [
            vmem(2, LANES, LANES),
            vmem(3, LAYERS, PADDED, LANES),
            vmem(3, LAYERS, PADDED, LANES),
            vmem(3, *block),
            vmem(5, *block),
            pltpu.VMEM(block, jnp.int32),
            vmem(1, LAYERS, PADDED, LANES),
            vmem(1, *tile),
            vmem(2, 1, *tile),
            vmem(3, *wide),
            vmem(3, ROWS, LANES),
            vmem(steps, *wide),
            vmem(steps, ROWS, LANES),
            vmem(steps, *block),
            vmem(steps, 6, *block),
            vmem(steps, 6, *block),
            vmem(2, *block),
            dma((24,)), dma((11,)),
            dma((2, 10)), dma((2, 10)), dma((2, 10)), dma((2, 10)),
            dma((4,)), dma((4,)),
        ],
        compiler_params=pltpu.CompilerParams(
            collective_id=0, has_side_effects=True, vmem_limit_bytes=40 * 1024 * 1024
        ),
    )(*operands)
    return pl.pallas_call(
        hand_over,
        out_shape=(
            pltpu.HBM(fwd.shape, f32),
            pltpu.HBM(block, f32),
            pltpu.HBM(block, f32),
        ),
        in_specs=[in_hbm] * 3,
        out_specs=(in_hbm,) * 3,
        scratch_shapes=[dma((3,))],
    )(*(pltpu.with_memory_space_constraint(r, pltpu.VMEM) for r in results))


def solution(mesh):
    state, cells = P(None, None, "gx", "gy"), P(None, "gx", "gy")
    return jax.shard_map(
        shards,
        mesh=mesh,
        in_specs=(state, state, cells, P(), P(), P(), P(), P()),
        out_specs=(state, cells, cells),
        check_vma=False,
    )
```

```python
import functools

import jax
import jax.numpy as jnp
from jax import lax
from jax.experimental import pallas as pl
from jax.experimental.pallas import tpu as pltpu
from jax.sharding import PartitionSpec as P

coeffs = (1225.0 / 1024.0, -245.0 / 3072.0, 49.0 / 5120.0, -5.0 / 7168.0)
step_dt = 0.1
MESH = pl.DeviceIdType.MESH

LAYERS, ROWS, LANES, SUB = 4, 16, 128, 8
REACH = 4
BASE = 16
PADDED = ROWS + 2 * BASE
END = BASE + ROWS

FWD = (3, 6, 7, 4, 8, 5, 0, 1, 2)
ADJ = (0, 1, 2, 3, 6, 7, 4, 8, 5)
FWD_EDGES = tuple(range(9))
ADJ_EDGES = (0, 1, 2, 4, 6, 7)
FWD_CORNERS = (1, 3, 4, 0, 2)
ADJ_CORNERS = (0, 1)


def place_in_grid():
    gx, gy = lax.axis_index("gx"), lax.axis_index("gy")
    return gx, gy, lax.axis_size("gx"), lax.axis_size("gy")


def neighbours():
    gx, gy, nx, ny = place_in_grid()
    xs = {-1: lax.rem(gx + nx - 1, nx), 0: gx, 1: lax.rem(gx + 1, nx)}
    ys = {-1: lax.rem(gy + ny - 1, ny), 0: gy, 1: lax.rem(gy + 1, ny)}
    in_x, in_y = {-1: gx > 0, 1: gx < nx - 1}, {-1: gy > 0, 1: gy < ny - 1}
    out = {}
    for dx in (-1, 0, 1):
        for dy in (-1, 0, 1):
            if dx and dy:
                out[dx, dy] = (xs[dx], ys[dy]), jnp.logical_and(in_x[dx], in_y[dy])
            elif dx or dy:
                out[dx, dy] = (xs[dx], ys[dy]), in_x[dx] if dx else in_y[dy]
    return out


def lane_of(shape):
    return lax.broadcasted_iota(jnp.int32, shape, len(shape) - 1)


def row_of(shape):
    return lax.broadcasted_iota(jnp.int32, shape, len(shape) - 2)


def roll(value, by):
    by %= LANES
    return value if by == 0 else pltpu.roll(value, by, value.ndim - 1)


def weighted(shift, plus):
    total = None
    for k in range(1, REACH + 1):
        first = k if plus else k - 1
        term = coeffs[k - 1] * (shift(first) - shift(first + 1 - 2 * k))
        total = term if total is None else total + term
    return total


def halo_rows(buf, field, d=0):
    after = buf[field, :, END + d : END + d + SUB, :]
    before = buf[field, :, BASE - SUB + d : BASE + d, :]
    return jnp.where(row_of(after.shape) < REACH, after, before)


def halo_diff_x(buf, field, plus):
    return weighted(lambda d: halo_rows(buf, field, d), plus)


def diff_x(buf, field, plus):
    return weighted(lambda d: buf[field, :, BASE + d : END + d, :], plus)


def near_and_far(shift, plus):
    sign = -1 if plus else 1
    taps = [shift(sign * k) for k in range(REACH)]
    near = far = None
    for k in range(REACH):
        one, two = coeffs[k] * taps[k], coeffs[REACH - 1 - k] * taps[k]
        near = one if near is None else near + one
        far = two if far is None else far + two
    return near, far


def ring_diff_y(field, plus):
    near, far = near_and_far(lambda d: roll(field, -d), plus)
    return roll(far, -REACH) - near if plus else near - roll(far, REACH)


def diff_z(field, plus):
    out = []
    for i in range(LAYERS):
        total = None
        for k in range(1, REACH + 1):
            first = i + (k if plus else k - 1)
            second = first + 1 - 2 * k
            has_first, has_second = 0 <= first < LAYERS, 0 <= second < LAYERS
            if has_first and has_second:
                term = coeffs[k - 1] * (field[first] - field[second])
            elif has_first:
                term = coeffs[k - 1] * field[first]
            elif has_second:
                term = -coeffs[k - 1] * field[second]
            else:
                continue
            total = term if total is None else total + term
        out.append(total)
    return jnp.stack(out)


def strip_x(buf, field, plus):
    return weighted(lambda d: buf[field, BASE + d : END + d, :], plus)


strip_y = ring_diff_y


def strip_z(field, plus):
    layer = lane_of(field.shape) // 32
    weights = {}
    for k in range(1, REACH + 1):
        first = k if plus else k - 1
        weights[first] = weights.get(first, 0.0) + coeffs[k - 1]
        weights[first + 1 - 2 * k] = weights.get(first + 1 - 2 * k, 0.0) - coeffs[k - 1]
    total = None
    for d, weight in weights.items():
        if abs(d) >= LAYERS:
            continue
        inside = (layer + d >= 0) & (layer + d < LAYERS)
        term = jnp.where(inside, weight, 0.0) * roll(field, -32 * d)
        total = term if total is None else total + term
    return total


def pack_edge(field):
    group = lane_of((SUB, LANES)) // 16
    packed = None
    for z in range(LAYERS):
        for tile in range(2):
            at = 2 * z + tile
            piece = roll(field[z, SUB * tile : SUB * (tile + 1)], 8 + 16 * at)
            packed = piece if packed is None else jnp.where(group == at, piece, packed)
    return packed


def pack_corners(edges, out_ref, slot):
    group = lane_of((SUB, LANES)) // 8 % 4
    top = row_of((SUB, LANES)) < REACH
    for start in range(0, len(edges), 4):
        packed = None
        for g, edge in enumerate(edges[start : start + 4]):
            piece = jnp.where(top, roll(edge, 8 * g - 4), roll(edge, 8 * g - 20))
            packed = piece if packed is None else jnp.where(group == g, piece, packed)
        out_ref[slot, start // 4] = packed


def strip_of(edge, low, high):
    half = lane_of(edge.shape) % 16 < 8
    first, last = jnp.where(half, low, edge), jnp.where(half, edge, high)
    side = lane_of(edge.shape) % 32 < 16
    tiles = [jnp.where(side, first, roll(last, 16)), jnp.where(side, roll(first, -16), last)]
    return jnp.concatenate(tiles, axis=0)


def end_terms(lack, plus):
    p = lane_of(lack.shape) % 16
    before, after = jnp.where(p < 8, lack, 0.0), jnp.where(p < 8, 0.0, lack)
    first_lanes = last_lanes = None
    for k in range(1, REACH + 1):
        first = k if plus else k - 1
        second = first + 1 - 2 * k
        if first > 0:
            term = coeffs[k - 1] * roll(after, -first)
            last_lanes = term if last_lanes is None else last_lanes + term
        if second < 0:
            term = coeffs[k - 1] * roll(before, -second)
            first_lanes = -term if first_lanes is None else first_lanes - term
    return jnp.where(p < 8, last_lanes, first_lanes)


def at_ends(value):
    lane = lane_of(value.shape)
    return jnp.where((lane < REACH) | (lane >= LANES - REACH), value, 0.0)


def ring_correction(edge, low, high, plus):
    total = end_terms(jnp.where(lane_of(edge.shape) % 16 < 8, low, high) - edge, plus)
    return jnp.stack([
        jnp.concatenate([at_ends(roll(total, 120 - 32 * z - 16 * t)) for t in range(2)], axis=0)
        for z in range(LAYERS)
    ])


def y_ends_of_strip(strip, plus):
    merged = jnp.where(lane_of(strip.shape) % 16 < 8, strip, roll(strip, -16))
    total = end_terms(merged, plus)
    return jnp.stack([at_ends(roll(total, 120 - 32 * z)) for z in range(LAYERS)])


def stencil_matrix(plus):
    source = lax.broadcasted_iota(jnp.int32, (LANES, LANES), 0)
    off = source - lane_of((LANES, LANES))
    total = jnp.zeros((LANES, LANES), jnp.float32)
    for k in range(1, REACH + 1):
        first = k if plus else k - 1
        total = jnp.where(off == first, coeffs[k - 1], total)
        total = jnp.where(off == first + 1 - 2 * k, -coeffs[k - 1], total)
    return total


def inner_diff_y(fields, matrix):
    shape = fields[0].shape
    rows = shape[0] * shape[1]
    stacked = jnp.concatenate([f.reshape(rows, LANES) for f in fields], axis=0)
    out = jnp.dot(
        stacked, matrix, precision=lax.Precision.HIGHEST, preferred_element_type=jnp.float32
    )
    return [out[i * rows : (i + 1) * rows].reshape(shape) for i in range(len(fields))]


def corner_end_terms(corner):
    first = lane_of(corner.shape) % 8 < 4
    before, after = jnp.where(first, corner, 0.0), jnp.where(first, 0.0, corner)
    back = [None] + [roll(before, k) for k in range(1, REACH + 1)]
    ahead = [None] + [roll(after, -k) for k in range(1, REACH + 1)]

    def total(terms, shift):
        pairs = [(c, terms[k]) for k, c in enumerate(coeffs, shift) if k > 0]
        return sum((c * term for c, term in pairs[1:]), pairs[0][0] * pairs[0][1])

    p_stencil = jnp.where(first, total(ahead, 1), -total(back, 0))
    m_stencil = jnp.where(first, total(ahead, 0), -total(back, 1))
    return p_stencil, m_stencil


def strip_rows_of_corners(corner, g):
    side = lane_of(corner.shape) % 32 < 16
    return jnp.where(side, roll(corner, 4 - 8 * g), roll(corner, 20 - 8 * g))


class Chain:
    def __init__(self, refs, around, deep, shallow, edges, corners):
        self.around = around
        (self.buf, self.edge, self.side, self.corner, self.corners_in,
         self.strips, self.send_sem, self.recv_sem) = refs
        self.deep, self.shallow = deep, shallow
        self.edges, self.corner_places = edges, corners

    def copies(self, slot):
        out = []

        def add(dx, dy, src, dst):
            to, goes = self.around[dx, dy]
            _, arrives = self.around[-dx, -dy]
            copy = pltpu.make_async_remote_copy(
                src_ref=src,
                dst_ref=dst,
                send_sem=self.send_sem.at[slot, len(out)],
                recv_sem=self.recv_sem.at[slot, len(out)],
                device_id=to,
                device_id_type=MESH,
            )
            out.append((goes, arrives, copy))

        for dx in (-1, 1):
            for dy in (-1, 1):
                at = (1 - dx) // 2 * 2 + (1 - dy) // 2
                add(dx, dy, self.corner.at[slot], self.corners_in.at[slot, at])
        for dy in (-1, 1):
            add(0, dy, self.edge.at[slot], self.side.at[slot, (1 - dy) // 2])
        for fields, count in ((self.deep, SUB), (self.shallow, REACH)):
            for dx in (-1, 1):
                src = BASE if dx < 0 else END - count
                dst = END if dx < 0 else BASE - count
                part = pl.ds(fields[0], len(fields))
                add(dx, 0, self.buf.at[slot, part, :, pl.ds(src, count), :],
                    self.buf.at[slot, part, :, pl.ds(dst, count), :])
        return out

    def clear(self):
        for slot in range(2):
            for fields, count in ((self.deep, SUB), (self.shallow, REACH)):
                zero = jnp.zeros((len(fields), LAYERS, count, LANES), jnp.float32)
                part = pl.ds(fields[0], len(fields))
                self.buf[slot, part, :, BASE - count : BASE, :] = zero
                self.buf[slot, part, :, END : END + count, :] = zero
        self.side[...] = jnp.zeros_like(self.side)
        self.corners_in[...] = jnp.zeros_like(self.corners_in)

    def pack(self, slot):
        edges = []
        for place in self.corner_places:
            edges.append(pack_edge(self.own(slot, place)))
            self.edge[slot, self.edges.index(place)] = edges[-1]
        pack_corners(edges, self.corner, slot)

    def pack_rest(self, slot):
        for i, place in enumerate(self.edges):
            if place not in self.corner_places:
                self.edge[slot, i] = pack_edge(self.own(slot, place))

    def start(self, slot, first, last):
        for goes, _, copy in self.copies(slot)[first:last]:
            pl.when(goes)(copy.start)

    def send(self, slot):
        self.pack(slot)
        self.start(slot, 0, 4)
        self.start(slot, 6, 10)
        self.pack_rest(slot)
        self.start(slot, 4, 6)

    def wait_recv(self, slot):
        for _, arrives, copy in self.copies(slot):
            pl.when(arrives)(copy.wait_recv)

    def wait_send(self, slot):
        for goes, _, copy in self.copies(slot):
            pl.when(goes)(copy.wait_send)

    def own(self, slot, place):
        return self.buf[slot, place, :, BASE:END, :]

    def put(self, slot, place, value):
        self.buf[slot, place, :, BASE:END, :] = value

    def strip(self, slot, place):
        i = self.edges.index(place)
        return strip_of(self.edge[slot, i], self.side[slot, 0, i], self.side[slot, 1, i])

    def ring_correction(self, slot, place, plus):
        i = self.edges.index(place)
        return ring_correction(
            self.edge[slot, i], self.side[slot, 0, i], self.side[slot, 1, i], plus
        )

    def corner_tiles(self, slot):
        shape = (SUB, LANES)
        first, top = lane_of(shape) % 8 < 4, row_of(shape) < REACH
        out = []
        for i in range(self.corner.shape[1]):
            here = [self.corners_in[slot, at, i] for at in range(4)]
            out.append(jnp.where(top, jnp.where(first, here[2], here[3]),
                                 jnp.where(first, here[0], here[1])))
        return out

    def corner_ends(self, place, totals):
        g = self.corner_places.index(place)
        return jnp.stack([at_ends(roll(totals, 124 - 32 * z - 8 * g)) for z in range(LAYERS)])

    def set_strip_rows(self, place, strip, tiles):
        at = self.corner_places.index(place)
        rows = strip_rows_of_corners(tiles[at // 4], at % 4)
        self.strips[place, BASE:END, :] = strip
        self.strips[place, BASE - SUB : BASE, :] = rows
        self.strips[place, END : END + SUB, :] = rows


def put_halo_rows(work, place, value):
    work[place, :, END : END + REACH, :] = value[:, :REACH]
    work[place, :, BASE - REACH : BASE, :] = value[:, REACH:]


def log2(n):
    assert n > 0 and n & (n - 1) == 0
    return n.bit_length() - 1


def spread(traces_ref, row, lane, rows, store):
    steps, count = traces_ref.shape
    row_hit = lax.broadcasted_iota(jnp.int32, (rows, count), 0) == row
    lane_hit = lax.broadcasted_iota(jnp.int32, (LANES, count), 0) == lane
    lanes = jnp.where(lane_hit, 1.0, 0.0).astype(jnp.bfloat16)
    for t in range(steps):
        rest = traces_ref[t : t + 1, :]
        total = None
        for _ in range(3):
            piece = rest.astype(jnp.bfloat16).astype(jnp.float32)
            rest = rest - piece
            left = jnp.where(row_hit, piece, 0.0).astype(jnp.bfloat16)
            part = lax.dot_general(
                left, lanes, (((1,), (1,)), ((), ())), preferred_element_type=jnp.float32
            )
            total = part if total is None else total + part
        store(t, step_dt * total)


def positions(cells_ref, nx_cells, ny_cells):
    gx, gy, _, _ = place_in_grid()
    cells = cells_ref[...]
    layer = lax.shift_right_logical(cells, jnp.int32(log2(nx_cells * ny_cells)))
    at_x = lax.shift_right_logical(cells, jnp.int32(log2(ny_cells))) & (nx_cells - 1)
    return layer, at_x - gx * ROWS, (cells & (ny_cells - 1)) - gy * LANES


def kernel(
    dims,
    fwd_hbm, adj_hbm, labels_hbm, table_hbm, src_hbm, wav_hbm, rec_hbm, res_hbm,
    out_ref, gl_ref, gm_ref,
    table_ref, src_ref, wav_ref, rec_ref, res_ref,
    f_buf, f_edge, f_side, f_corner, f_corners_in, f_strips,
    a_buf, a_edge, a_side, a_corner, a_corners_in, a_strips,
    matrices, f_work, a_work, f_part, a_part, labels, lab, lab_edge, lab_side, mats, mats_s,
    inj_f, inj_s, inj_a, e_all, f_all, grads,
    in_sem, out_sem, f_send, f_recv, a_send, a_recv, l_send, l_recv,
):
    nx_cells, ny_cells = dims
    gx, gy, nx, ny = place_in_grid()
    steps = wav_ref.shape[0]

    around = neighbours()
    fwd = Chain((f_buf, f_edge, f_side, f_corner, f_corners_in, f_strips, f_send, f_recv),
                around, (0, 1, 2), (3, 4, 5, 6, 7, 8), FWD_EDGES, FWD_CORNERS)
    adj = Chain((a_buf, a_edge, a_side, a_corner, a_corners_in, a_strips, a_send, a_recv),
                around, (0, 1, 2), (3, 4, 5), ADJ_EDGES, ADJ_CORNERS)

    fwd.clear()
    adj.clear()
    lab[...] = jnp.zeros_like(lab)
    lab_side[...] = jnp.zeros_like(lab_side)
    barrier = pltpu.get_barrier_semaphore()
    for to, _ in around.values():
        pl.semaphore_signal(barrier, inc=1, device_id=to, device_id_type=MESH)

    loads = []

    def load(src, dst):
        copy = pltpu.make_async_copy(src, dst, in_sem.at[len(loads)])
        copy.start()
        loads.append(copy)

    own_rows = pl.ds(BASE, ROWS)
    load(labels_hbm, labels)
    for hbm, buf, order in ((fwd_hbm, f_buf, FWD), (adj_hbm, a_buf, ADJ)):
        start = 0
        for end in range(1, len(order) + 1):
            if end == len(order) or order[end] != order[end - 1] + 1:
                part = pl.ds(order[start], end - start)
                load(hbm.at[part], buf.at[0, pl.ds(start, end - start), :, own_rows, :])
                start = end
    first = len(loads)
    for src, dst in (
        (table_hbm, table_ref), (src_hbm, src_ref), (wav_hbm, wav_ref),
        (rec_hbm, rec_ref), (res_hbm, res_ref),
    ):
        load(src, dst)

    loads[0].wait()
    lab[0, :, BASE:END, :] = labels[...].astype(jnp.float32)
    lab_edge[0] = pack_edge(lab[0, :, BASE:END, :])
    lab_copies = []
    own_labels = lab.at[0]
    for dx, dy, src, dst in (
        (-1, 0, own_labels.at[:, pl.ds(BASE, REACH), :], own_labels.at[:, pl.ds(END, REACH), :]),
        (1, 0, own_labels.at[:, pl.ds(END - REACH, REACH), :], own_labels.at[:, pl.ds(BASE - REACH, REACH), :]),
        (0, -1, lab_edge, lab_side.at[1]),
        (0, 1, lab_edge, lab_side.at[0]),
    ):
        to, goes = around[dx, dy]
        copy = pltpu.make_async_remote_copy(
            src_ref=src, dst_ref=dst, send_sem=l_send.at[len(lab_copies)],
            recv_sem=l_recv.at[len(lab_copies)], device_id=to, device_id_type=MESH,
        )
        lab_copies.append((goes, around[-dx, -dy][1], copy))

    for copy in loads[1:first]:
        copy.wait()
    for chain in (fwd, adj):
        chain.pack(0)
        chain.pack_rest(0)
    pl.semaphore_wait(barrier, len(around))
    fwd.start(0, 0, 6)
    adj.start(0, 0, 6)
    for goes, _, copy in lab_copies:
        pl.when(goes)(copy.start)
    fwd.start(0, 6, 10)
    adj.start(0, 6, 10)

    for copy in loads[first:]:
        copy.wait()
    layer, at_x, at_y = positions(src_ref, nx_cells, ny_cells)
    wide = ROWS + SUB
    here = jnp.where(at_x < 0, at_x + wide, at_x)
    row = jnp.where((at_x >= -REACH) & (at_x < ROWS + REACH), layer * wide + here, -1)

    def store_wide(t, value):
        inj_f[t] = value.reshape(LAYERS, wide, LANES)

    spread(wav_ref, row, at_y, LAYERS * wide, store_wide)
    column = jnp.where((at_y >= -REACH) & (at_y < 0), 32 * layer + 8 + at_y, -1)
    column = jnp.where((at_y >= LANES) & (at_y < LANES + REACH), 32 * layer + 24 + at_y - LANES, column)

    def store_strip(t, value):
        inj_s[t] = value

    spread(wav_ref, at_x, column, ROWS, store_strip)
    layer, at_x, at_y = positions(rec_ref, nx_cells, ny_cells)
    row = jnp.where((at_x >= 0) & (at_x < ROWS), layer * ROWS + at_x, -1)

    def store_own(t, value):
        inj_a[t] = value.reshape(LAYERS, ROWS, LANES)

    spread(res_ref, row, at_y, LAYERS * ROWS, store_own)

    matrices[0] = stencil_matrix(True)
    matrices[1] = stencil_matrix(False)

    for _, arrives, copy in lab_copies:
        pl.when(arrives)(copy.wait_recv)

    def materials(label, inside, out):
        for prop in range(3):
            value = jnp.full(label.shape, table_ref[prop, 0])
            for phase in range(1, table_ref.shape[1]):
                value = jnp.where(label == phase, table_ref[prop, phase], value)
            value = step_dt * value if prop < 2 else step_dt / value
            out[prop] = jnp.where(inside, value, 0.0)

    shape = (LAYERS, wide, LANES)
    r = row_of(shape)
    inside = (r < ROWS) | ((r < ROWS + REACH) & (gx < nx - 1)) | ((r >= ROWS + REACH) & (gx > 0))
    both = jnp.concatenate([lab[0, :, BASE:END, :], halo_rows(lab, 0)], axis=1)
    materials(both, inside, mats)
    lane = lane_of((ROWS, LANES))
    column = lane % 16 + jnp.where(lane % 32 < 16, -8, LANES - 8)
    inside = ((column >= 0) | (gy > 0)) & ((column < LANES) | (gy < ny - 1))
    materials(strip_of(lab_edge[0], lab_side[0, 0], lab_side[1, 0]), inside, mats_s)

    own_mats = lambda prop: mats[prop, :, :ROWS]
    halo_mats = lambda prop: mats[prop, :, ROWS:]
    sxx, sxy, sxz, syy, syz, szz, vx, vy, vz = range(9)
    f_terms = (
        ((sxx, True), (sxy, False), (sxz, False)),
        ((sxy, False), (syy, True), (syz, False)),
        ((sxz, False), (syz, False), (szz, True)),
    )

    def forward_ahead(t):
        slot = t % 2
        if t > 0:
            fwd.wait_send(1 - slot)
        for i, (_, (y, y_plus), (z, z_plus)) in enumerate(f_terms):
            terms = ring_diff_y(fwd.own(slot, y), y_plus) + diff_z(fwd.own(slot, z), z_plus)
            part = fwd.own(slot, vx + i) + own_mats(2) * terms
            f_part[i] = part + inj_f[t, :, :ROWS] if i == 2 else part

    def forward_step(t):
        slot, other = t % 2, 1 - t % 2
        buf = f_buf.at[slot]
        fwd.wait_recv(slot)
        tiles = fwd.corner_tiles(slot)
        strips = {}

        def strip(place):
            if place not in strips:
                strips[place] = fwd.strip(slot, place)
            return strips[place]

        for place in (sxx, sxy, sxz):
            fwd.set_strip_rows(place, strip(place), tiles)
        p_ends, m_ends = corner_end_terms(tiles[0])
        halo_y = dict(zip((syy,), inner_diff_y((halo_rows(buf, syy),), matrices[0])))
        halo_y.update(zip((sxy, syz), inner_diff_y(
            (halo_rows(buf, sxy), halo_rows(buf, syz)), matrices[1])))
        v, ends = [], []
        for i, ((x, x_plus), (y, y_plus), (z, z_plus)) in enumerate(f_terms):
            terms = diff_x(buf, x, x_plus) + fwd.ring_correction(slot, y, y_plus)
            v.append(f_part[i] + own_mats(2) * terms)
            fwd.put(other, vx + i, v[i])
            f_work[i, :, BASE:END, :] = v[i]
            terms = (
                halo_diff_x(buf, x, x_plus)
                + halo_y[y] + fwd.corner_ends(y, p_ends if y_plus else m_ends)
                + diff_z(halo_rows(buf, z), z_plus)
            )
            new = halo_rows(buf, vx + i) + halo_mats(2) * terms
            put_halo_rows(f_work, i, new + inj_f[t, :, ROWS:] if i == 2 else new)
            terms = (
                strip_x(f_strips, x, x_plus)
                + strip_y(strip(y), y_plus)
                + strip_z(strip(z), z_plus)
            )
            side = strip(vx + i) + mats_s[2] * terms
            ends.append(y_ends_of_strip(side + inj_s[t] if i == 2 else side, i != 1))
        vx_y, vz_y = inner_diff_y((v[0], v[2]), matrices[0])
        (vy_y,) = inner_diff_y((v[1],), matrices[1])
        strain = (
            diff_x(f_work, 0, False),
            vy_y + ends[1],
            diff_z(v[2], False),
            vx_y + ends[0] + diff_x(f_work, 1, True),
            diff_z(v[0], True) + diff_x(f_work, 2, True),
            diff_z(v[1], True) + vz_y + ends[2],
        )
        for i in range(6):
            e_all[t, i] = strain[i]
        if t < steps - 1:
            lam, shear = own_mats(0), own_mats(1)
            exx, eyy, ezz, exy, exz, eyz = strain
            base, twice = lam * (exx + eyy + ezz), 2.0 * shear
            for place, inc in (
                (sxx, base + twice * exx), (sxy, shear * exy), (sxz, shear * exz),
                (syy, base + twice * eyy), (syz, shear * eyz), (szz, base + twice * ezz),
            ):
                fwd.put(other, place, fwd.own(slot, place) + inc)
            fwd.send(other)

    ux, uy, uz, qxx, qxy, qxz, qyy, qyz, qzz = range(9)

    def adjoint_ahead(t):
        if t > 0:
            adj.wait_send(1 - t % 2)
        u = [adj.own(t % 2, i) for i in range(3)]
        a_part[0] = ring_diff_y(u[1], False)
        a_part[1] = diff_z(u[2], False)
        a_part[2] = ring_diff_y(u[0], True)
        a_part[3] = diff_z(u[0], True)
        a_part[4] = diff_z(u[1], True) + ring_diff_y(u[2], True)

    def adjoint_step(t):
        slot, other = t % 2, 1 - t % 2
        buf = a_buf.at[slot]
        adj.wait_recv(slot)
        tiles = adj.corner_tiles(slot)

        def put(place, value):
            if t < steps - 1:
                adj.put(other, place, value)
            else:
                out_ref[ADJ[place]] = value

        side = [adj.strip(slot, i) for i in range(3)]
        for i in range(2):
            adj.set_strip_rows(i, side[i], tiles)
        xx, yy, zz = strip_x(a_strips, ux, False), strip_y(side[1], False), strip_z(side[2], False)
        xy = strip_y(side[0], True) + strip_x(a_strips, uy, True)
        yz = strip_z(side[1], True) + strip_y(side[2], True)
        lam, shear = mats_s[0], mats_s[1]
        ends = {}
        for place, inc in (
            (qxy, shear * xy), (qyy, lam * (xx + yy + zz) + 2.0 * shear * yy), (qyz, shear * yz)
        ):
            ends[place] = y_ends_of_strip(adj.strip(slot, place) - inc, place == qyy)
        u = [halo_rows(buf, i) for i in range(3)]
        p_ends, m_ends = corner_end_terms(tiles[0])
        (ux_y,), (uy_y,) = inner_diff_y((u[0],), matrices[0]), inner_diff_y((u[1],), matrices[1])
        exx, eyy = halo_diff_x(buf, ux, False), uy_y + adj.corner_ends(uy, m_ends)
        exy = ux_y + adj.corner_ends(ux, p_ends) + halo_diff_x(buf, uy, True)
        exz = diff_z(u[0], True) + halo_diff_x(buf, uz, True)
        lam, shear = halo_mats(0), halo_mats(1)
        base = lam * (exx + eyy + diff_z(u[2], False))
        for i, (place, inc) in enumerate(
            ((qxx, base + 2.0 * shear * exx), (qxy, shear * exy), (qxz, shear * exz))
        ):
            put_halo_rows(a_work, i, halo_rows(buf, place) - inc)
        exx, ezz = diff_x(buf, ux, False), a_part[1]
        eyy = a_part[0] + adj.ring_correction(slot, uy, False)
        exy = a_part[2] + adj.ring_correction(slot, ux, True) + diff_x(buf, uy, True)
        exz = a_part[3] + diff_x(buf, uz, True)
        eyz = a_part[4] + adj.ring_correction(slot, uz, True)
        for i, value in enumerate((exx, eyy, ezz, exy, exz, eyz)):
            f_all[t, i] = value
        lam, shear = own_mats(0), own_mats(1)
        base, twice = lam * (exx + eyy + ezz), 2.0 * shear
        q = {}
        for place, inc in (
            (qxx, base + twice * exx), (qxy, shear * exy), (qxz, shear * exz),
            (qyy, base + twice * eyy), (qyz, shear * eyz), (qzz, base + twice * ezz),
        ):
            q[place] = adj.own(slot, place) - inc
            put(place, q[place])
        for i, place in enumerate((qxx, qxy, qxz)):
            a_work[i, :, BASE:END, :] = q[place]
        (qyy_y,) = inner_diff_y((q[qyy],), matrices[0])
        qxy_y, qyz_y = inner_diff_y((q[qxy], q[qyz]), matrices[1])
        div = (
            diff_x(a_work, 0, True) + qxy_y + ends[qxy] + diff_z(q[qxz], False),
            diff_x(a_work, 1, False) + qyy_y + ends[qyy] + diff_z(q[qyz], False),
            diff_x(a_work, 2, False) + qyz_y + ends[qyz] + diff_z(q[qzz], True),
        )
        for i in range(3):
            value = adj.own(slot, i) - own_mats(2) * div[i]
            put(i, value + inj_a[t] if i == 2 else value)
        if t < steps - 1:
            adj.send(other)

    for t in range(steps):
        forward_ahead(t)
        adjoint_ahead(t)
        forward_step(t)
        adjoint_step(t)

    last = (steps - 1) % 2
    fwd.wait_send(last)
    adj.wait_send(last)
    for goes, _, copy in lab_copies:
        pl.when(goes)(copy.wait_send)

    grad_l = grad_m = None
    for t in range(steps):
        e = [e_all[steps - 1 - t, i] for i in range(6)]
        f = [f_all[t, i] for i in range(6)]
        more_l = (e[0] + e[1] + e[2]) * (f[0] + f[1] + f[2])
        more_m = 2.0 * (e[0] * f[0] + e[1] * f[1] + e[2] * f[2])
        more_m = more_m + e[3] * f[3] + e[4] * f[4] + e[5] * f[5]
        grad_l = more_l if grad_l is None else grad_l + more_l
        grad_m = more_m if grad_m is None else grad_m + more_m
    gl_ref[...] = step_dt * grad_l
    gm_ref[...] = step_dt * grad_m


def hand_over(*refs):
    sem = refs[-1]
    copies = [pltpu.make_async_copy(refs[i], refs[3 + i], sem.at[i]) for i in range(3)]
    for copy in copies:
        copy.start()
    for copy in copies:
        copy.wait()


def shards(fwd, adj, labels, table, src, wav, rec, res):
    assert labels.shape == (LAYERS, ROWS, LANES)
    dims = (ROWS * lax.axis_size("gx"), LANES * lax.axis_size("gy"))
    steps = wav.shape[0]
    f32 = jnp.float32
    block, tile = (LAYERS, ROWS, LANES), (SUB, LANES)
    wide = (LAYERS, ROWS + SUB, LANES)

    def vmem(*shape):
        return pltpu.VMEM(shape, f32)

    def chain(edges, corners, strips):
        return [
            vmem(2, 9, LAYERS, PADDED, LANES),
            vmem(2, edges, *tile),
            vmem(2, 2, edges, *tile),
            vmem(2, corners, *tile),
            vmem(2, 4, corners, *tile),
            vmem(strips, PADDED, LANES),
        ]

    in_hbm = pl.BlockSpec(memory_space=pl.ANY)
    in_vmem = pl.BlockSpec(memory_space=pltpu.VMEM)
    dma = pltpu.SemaphoreType.DMA
    operands = [
        pltpu.with_memory_space_constraint(x, pltpu.HBM)
        for x in (fwd, adj, labels, table, src.reshape(1, -1), wav, rec.reshape(1, -1), res)
    ]
    results = pl.pallas_call(
        functools.partial(kernel, dims),
        out_shape=(
            pltpu.VMEM(fwd.shape, f32),
            pltpu.VMEM(block, f32),
            pltpu.VMEM(block, f32),
        ),
        in_specs=[in_hbm] * 8,
        out_specs=(in_vmem, in_vmem, in_vmem),
        scratch_shapes=[
            pltpu.SMEM(table.shape, f32),
            pltpu.VMEM((1,) + src.shape, jnp.int32),
            vmem(*wav.shape),
            pltpu.VMEM((1,) + rec.shape, jnp.int32),
            vmem(*res.shape),
        ] + chain(9, 2, 3) + chain(6, 1, 2) + [
            vmem(2, LANES, LANES),
            vmem(3, LAYERS, PADDED, LANES),
            vmem(3, LAYERS, PADDED, LANES),
            vmem(3, *block),
            vmem(5, *block),
            pltpu.VMEM(block, jnp.int32),
            vmem(1, LAYERS, PADDED, LANES),
            vmem(1, *tile),
            vmem(2, 1, *tile),
            vmem(3, *wide),
            vmem(3, ROWS, LANES),
            vmem(steps, *wide),
            vmem(steps, ROWS, LANES),
            vmem(steps, *block),
            vmem(steps, 6, *block),
            vmem(steps, 6, *block),
            vmem(2, *block),
            dma((24,)), dma((11,)),
            dma((2, 10)), dma((2, 10)), dma((2, 10)), dma((2, 10)),
            dma((4,)), dma((4,)),
        ],
        compiler_params=pltpu.CompilerParams(
            collective_id=0, has_side_effects=True, vmem_limit_bytes=40 * 1024 * 1024
        ),
    )(*operands)
    return pl.pallas_call(
        hand_over,
        out_shape=(
            pltpu.HBM(fwd.shape, f32),
            pltpu.HBM(block, f32),
            pltpu.HBM(block, f32),
        ),
        in_specs=[in_hbm] * 3,
        out_specs=(in_hbm,) * 3,
        scratch_shapes=[dma((3,))],
    )(*(pltpu.with_memory_space_constraint(r, pltpu.VMEM) for r in results))


def solution(mesh):
    state, cells = P(None, None, "gx", "gy"), P(None, "gx", "gy")
    return jax.shard_map(
        shards,
        mesh=mesh,
        in_specs=(state, state, cells, P(), P(), P(), P(), P()),
        out_specs=(state, cells, cells),
        check_vma=False,
    )
```
